32 devices in a mesh: seq: 8 (over z, x), tp: 4 (over y, core).
Axes of the slice: x: 2, y: 2, z: 4, core: 2. Of those that a mesh axis runs over, the one named last changes fastest.
Arguments:
- queries: bfloat16 [2048, 8192], P('seq', 'tp'), may hold values from -1000 to 1000
- states: bfloat16 [4096, 4096], P('seq', 'tp'), may hold values from -18 to 18
- state_doc: int32 [4096], replicated, may hold values from 0 to 7, as said below
- state_pos: int32 [4096], replicated, may hold values from 0 to 511, as said below
- lengths: int32 [8], replicated, may hold values from 64 to 512, as said below
- offsets: int32 [8], replicated, may hold values from 0 to 256
- key_weight: bfloat16 [4096, 8192], P(None, 'tp'), may hold values from -1 to 1
- value_weight: bfloat16 [4096, 8192], P(None, 'tp'), may hold values from -1 to 1
- context_grad: bfloat16 [2048, 8192], P('seq', 'tp'), may hold values from -6 to 6
Outputs:
- query_grad: bfloat16 [2048, 8192], P('seq', 'tp')
- key_weight_grad: bfloat16 [4096, 8192], P('seq', 'tp')
- value_weight_grad: bfloat16 [4096, 8192], P('seq', 'tp')
The draws below stay inside these ranges and needn't reach their ends.
Inputs may be any that keep to these rules, and one draw needn't show every extreme that they name: `state_doc`: each document has exactly 512 state rows. The 512 rows held by one index of seq name any one document at most 80 times, and in every draw some device's rows name some document exactly 80 times. `state_pos`: within one document the state rows carry each position from 0 to 511 exactly once. `lengths`: some document has length 512.
All inputs are finite; a program needn't handle non-finite values.
Results may differ from the reference program's by a relative error of at most 0.017.
Values may be sent and summed in bfloat16 or wider, within the bound.
No kernel may reach another device: no remote copies, remote signals or barrier semaphores. Data moves between devices by JAX's collectives and lax.ppermute only.
A program may use at most 128 MiB of HBM per device.

```python
import jax
import jax.numpy as jnp
from jax import lax

D = 8192
HEADS = 64
HEAD_DIM = 128
DA = 4096
QDOC = 256
LDOC = 512
NDOC = 8
TOKENS = 2048
S_ROWS = 4096


def shuffle_one(subkey):
    return jax.random.permutation(subkey, LDOC)


def route_table(key):
    sigma = jax.random.permutation(jax.random.fold_in(key, 11), NDOC)
    base_count = 3 * LDOC // (4 * NDOC)
    lift_count = LDOC // 16
    nudge_count = base_count // 2
    sources = jnp.arange(NDOC)
    counts = jnp.full((NDOC, NDOC), base_count, jnp.int32)
    for step_shift, amount in ((0, lift_count), (1, lift_count), (2, lift_count), (3, lift_count), (4, nudge_count), (5, -nudge_count)):
        counts = counts.at[sources, sigma[(sources + step_shift) % NDOC]].add(amount)
    bounds = jnp.cumsum(counts, axis=1)
    slot_index = jnp.arange(LDOC)
    doc_of = jnp.sum((slot_index[None, :, None] >= bounds[:, None, :]).astype(jnp.int32), axis=2)
    shuffles = jax.vmap(shuffle_one)(jax.random.split(jax.random.fold_in(key, 12), NDOC))
    docs = jnp.take_along_axis(doc_of, shuffles, axis=1).reshape(-1)
    onehot = (docs[:, None] == jnp.arange(NDOC)[None, :]).astype(jnp.int32)
    ranks = jnp.sum((jnp.cumsum(onehot, axis=0) - onehot) * onehot, axis=1)
    position_perm = jax.vmap(shuffle_one)(jax.random.split(jax.random.fold_in(key, 13), NDOC))
    positions = position_perm[docs, ranks]
    return (docs.astype(jnp.int32), positions.astype(jnp.int32))


def state_table(key):
    docs, positions = route_table(key)
    raw_values = jnp.clip(jax.random.normal(jax.random.fold_in(key, 31), (S_ROWS, DA), jnp.float32), -6.0, 6.0)
    pairing = jax.random.permutation(jax.random.fold_in(key, 32), NDOC)
    column_block = jnp.arange(DA) // (DA // NDOC)
    boost = 1.0 + 2.0 * (column_block[None, :] == pairing[docs][:, None]).astype(jnp.float32)
    return raw_values * boost


def weight_table(key, salt):
    raw_values = jnp.clip(jax.random.normal(jax.random.fold_in(key, salt), (DA, D), jnp.float32), -6.0, 6.0)
    return (raw_values * DA ** (-0.5)).astype(jnp.bfloat16)


def draw_state_doc(key, part):
    return route_table(key)[0]


def draw_state_pos(key, part):
    return route_table(key)[1]


def draw_lengths(key, part):
    drawn = jax.random.randint(jax.random.fold_in(key, 21), (NDOC,), LDOC // 8, LDOC + 1)
    chosen = jax.random.randint(jax.random.fold_in(key, 22), (), 0, NDOC)
    return drawn.at[chosen].set(LDOC).astype(jnp.int32)


def draw_states(key, part):
    return state_table(key).astype(jnp.bfloat16)


def draw_key_weight(key, part):
    return weight_table(key, 41)


def draw_value_weight(key, part):
    return weight_table(key, 42)


def draw_context_grad(key, part):
    result = jnp.clip(jax.random.normal(jax.random.fold_in(key, 61), (TOKENS, D), jnp.float32), -6.0, 6.0)
    return result.astype(jnp.bfloat16)


def draw_queries(key, part):
    result = jnp.clip(jax.random.normal(jax.random.fold_in(key, 51), (TOKENS, D), jnp.float32), -6.0, 6.0)
    return jnp.clip(result, -1000.0, 1000.0).astype(jnp.bfloat16)


def place_ends(values, own_key, least, high):
    shape = values.shape
    place = [jax.random.randint(jax.random.fold_in(own_key, axis), (), 0, shape[axis]) for axis in range(len(shape))]
    values = values.at[tuple(place)].set(least)
    longest = shape.index(max(shape))
    place[longest] = (place[longest] + 1) % shape[longest]
    return values.at[tuple(place)].set(high)


def setup_inputs(seed: int = 0) -> dict:
    key_of = jax.random.split(jax.random.key(seed), 10)
    return {
        "queries": draw_queries(jax.random.fold_in(key_of[9], 71), 0),
        "states": draw_states(jax.random.fold_in(key_of[9], 71), 0),
        "state_doc": draw_state_doc(jax.random.fold_in(key_of[9], 71), 0),
        "state_pos": draw_state_pos(jax.random.fold_in(key_of[9], 71), 0),
        "lengths": draw_lengths(jax.random.fold_in(key_of[9], 71), 0),
        "offsets": place_ends(jax.random.randint(key_of[5], (NDOC,), 0, LDOC - QDOC + 1), jax.random.fold_in(key_of[5], 1), 0, LDOC - QDOC).astype(jnp.int32),
        "key_weight": draw_key_weight(jax.random.fold_in(key_of[9], 71), 0),
        "value_weight": draw_value_weight(jax.random.fold_in(key_of[9], 71), 0),
        "context_grad": draw_context_grad(jax.random.fold_in(key_of[9], 71), 0),
    }


def attend(query_rows, state_rows, positions, length, offset, key_weight, value_weight, grad_rows):
    key_rows = jnp.dot(state_rows, key_weight, preferred_element_type=jnp.float32).astype(jnp.bfloat16)
    value_rows = jnp.dot(state_rows, value_weight, preferred_element_type=jnp.float32).astype(jnp.bfloat16)
    query_count = query_rows.shape[0]
    state_count = state_rows.shape[0]
    query_heads = query_rows.reshape(query_count, HEADS, HEAD_DIM).astype(jnp.float32)
    key_heads = key_rows.reshape(state_count, HEADS, HEAD_DIM).astype(jnp.float32)
    value_heads = value_rows.reshape(state_count, HEADS, HEAD_DIM).astype(jnp.float32)
    grad_heads = grad_rows.reshape(query_count, HEADS, HEAD_DIM).astype(jnp.float32)
    score_scale = HEAD_DIM ** -0.5
    scores = jnp.einsum("qhd,khd->hqk", query_heads, key_heads) * score_scale
    query_index = jnp.arange(query_count)
    visible = (positions[None, :] <= offset + query_index[:, None]) & (positions[None, :] < length)
    scores = jnp.where(visible[None], scores, -jnp.inf)
    row_top = jnp.max(scores, axis=-1, keepdims=True)
    weights = jnp.exp(scores - row_top)
    probabilities = weights / jnp.sum(weights, axis=-1, keepdims=True)
    probs_low = probabilities.astype(jnp.bfloat16)
    probs_wide = probs_low.astype(jnp.float32)
    context = jnp.einsum("hqk,khd->qhd", probs_wide, value_heads)
    delta_rows = jnp.sum(grad_heads * context, axis=-1)
    prob_grad = jnp.einsum("qhd,khd->hqk", grad_heads, value_heads)
    score_grad = (probabilities * (prob_grad - delta_rows.T[:, :, None]) * score_scale).astype(jnp.bfloat16)
    score_wide = score_grad.astype(jnp.float32)
    query_grad = jnp.einsum("hqk,khd->qhd", score_wide, key_heads).astype(jnp.bfloat16)
    key_grad = jnp.einsum("hqk,qhd->khd", score_wide, query_heads).astype(jnp.bfloat16)
    value_grad = jnp.einsum("hqk,qhd->khd", probs_wide, grad_heads).astype(jnp.bfloat16)
    return (query_grad.reshape(query_count, D), key_grad.reshape(state_count, D),
            value_grad.reshape(state_count, D))


def reference(queries, states, state_doc, state_pos, lengths, offsets, key_weight, value_weight, context_grad):
    order = jnp.argsort(state_doc, stable=True)
    doc_states = jnp.take(states, order, axis=0).reshape(NDOC, LDOC, DA)
    doc_positions = jnp.take(state_pos, order, axis=0).reshape(NDOC, LDOC)
    doc_queries = queries.reshape(NDOC, QDOC, D)
    doc_grads = context_grad.reshape(NDOC, QDOC, D)

    def visit(totals, item):
        state_rows, positions, query_rows, grad_rows, length, offset = item
        query_grad, key_grad, value_grad = attend(query_rows, state_rows, positions, length, offset,
                                                  key_weight, value_weight, grad_rows)
        key_part = jnp.dot(state_rows.T, key_grad, preferred_element_type=jnp.float32).astype(jnp.bfloat16)
        value_part = jnp.dot(state_rows.T, value_grad, preferred_element_type=jnp.float32).astype(jnp.bfloat16)
        key_part, value_part = lax.optimization_barrier((key_part, value_part))
        return (totals[0] + key_part.astype(jnp.float32), totals[1] + value_part.astype(jnp.float32)), query_grad

    zeros = jnp.zeros((DA, D), jnp.float32)
    totals, query_grads = lax.scan(visit, (zeros, zeros),
                                   (doc_states, doc_positions, doc_queries, doc_grads, lengths, offsets))
    return (query_grads.reshape(TOKENS, D), totals[0].astype(jnp.bfloat16), totals[1].astype(jnp.bfloat16))
```

```python
import jax
import jax.numpy as jnp
from jax import lax
from jax.experimental import pallas as pl
from jax.experimental.pallas import tpu as pltpu
from jax.sharding import PartitionSpec as P

HEAD_DIM = 128
LOW = jnp.bfloat16
WIDE = jnp.float32


def attend_kernel(info_ref, query_ref, key_ref, value_ref, grad_ref, query_grad_ref, rows_grad_ref):
    head = pl.program_id(0)
    length = info_ref[0]
    offset = info_ref[1]
    scale = HEAD_DIM ** (-0.5)
    query, key, value, grad = query_ref[...], key_ref[...], value_ref[...], grad_ref[...]
    across = (((1,), (1,)), ((), ()))
    down = (((0,), (0,)), ((), ()))
    scores = lax.dot_general(query, key, across, preferred_element_type=WIDE) * scale
    position = lax.broadcasted_iota(jnp.int32, scores.shape, 1)
    limit = jnp.minimum(
        lax.broadcasted_iota(jnp.int32, (scores.shape[0], 1), 0) + (offset + 1), length
    )
    scores = jnp.where(position < limit, scores, -1e30)
    weights = jnp.exp(scores - jnp.max(scores, axis=-1, keepdims=True))
    probs = weights * (1.0 / jnp.sum(weights, axis=-1, keepdims=True))
    probs_low = probs.astype(LOW)
    context = jnp.dot(probs_low, value, preferred_element_type=WIDE)
    delta = jnp.sum(grad.astype(WIDE) * context, axis=-1, keepdims=True)
    prob_grad = lax.dot_general(grad, value, across, preferred_element_type=WIDE)
    score_grad = (probs * (prob_grad - delta) * scale).astype(LOW)
    query_grad_ref[...] = jnp.dot(score_grad, key, preferred_element_type=WIDE).astype(LOW)
    key_grad = lax.dot_general(score_grad, query, down, preferred_element_type=WIDE)
    value_grad = lax.dot_general(probs_low, grad, down, preferred_element_type=WIDE)
    half = rows_grad_ref.shape[1] // 2
    start = pl.multiple_of(head * HEAD_DIM, HEAD_DIM)
    rows_grad_ref[:, pl.ds(start, HEAD_DIM)] = key_grad.astype(LOW)
    rows_grad_ref[:, pl.ds(half + start, HEAD_DIM)] = value_grad.astype(LOW)


def attend(info, queries, key_rows, value_rows, grads, first, heads):
    query_count = queries.shape[0]
    state_count = key_rows.shape[0]
    width = heads * HEAD_DIM
    flops = 12 * query_count * state_count * width
    return pl.pallas_call(
        attend_kernel,
        grid=(heads,),
        in_specs=[
            pl.BlockSpec(memory_space=pltpu.SMEM),
            pl.BlockSpec((query_count, HEAD_DIM), lambda h: (0, first + h)),
            pl.BlockSpec((state_count, HEAD_DIM), lambda h: (0, h)),
            pl.BlockSpec((state_count, HEAD_DIM), lambda h: (0, h)),
            pl.BlockSpec((query_count, HEAD_DIM), lambda h: (0, first + h)),
        ],
        out_specs=[
            pl.BlockSpec((query_count, HEAD_DIM), lambda h: (0, h)),
            pl.BlockSpec((state_count, 2 * width), lambda h: (0, 0)),
        ],
        out_shape=[
            jax.ShapeDtypeStruct((query_count, width), LOW),
            jax.ShapeDtypeStruct((state_count, 2 * width), LOW),
        ],
        compiler_params=pltpu.CompilerParams(vmem_limit_bytes=24 * 1024 * 1024),
        cost_estimate=pl.CostEstimate(
            flops=4 * flops, bytes_accessed=12 * state_count * width, transcendentals=query_count * state_count * heads
        ),
    )(info, queries, key_rows, value_rows, grads)


def down_dot(left, right):
    return lax.dot_general(left, right, (((0,), (0,)), ((), ())), preferred_element_type=WIDE)


def line_shape(seq_count):
    minor = 1
    while (2 * minor) ** 2 <= seq_count and seq_count % (2 * minor) == 0:
        minor *= 2
    return seq_count // minor, minor


def route(states, state_doc, state_pos):
    seq_count = lax.axis_size("seq")
    device = lax.axis_index("seq")
    row_count = states.shape[0]
    capacity = 3 * row_count // (4 * seq_count) + row_count // 16
    docs_all = state_doc.reshape(seq_count, row_count)
    positions_all = state_pos.reshape(seq_count, row_count)
    before = (
        lax.broadcasted_iota(jnp.int32, (row_count, row_count), 0)
        < lax.broadcasted_iota(jnp.int32, (row_count, row_count), 1)
    ).astype(LOW)
    own_docs = lax.dynamic_index_in_dim(docs_all, device, 0, keepdims=False)
    doc_ids = jnp.arange(seq_count, dtype=jnp.int32)
    own_hot = own_docs[None, :] == doc_ids[:, None]
    mine = docs_all == device
    ranks = jnp.dot(
        jnp.concatenate([own_hot, mine], axis=0).astype(LOW), before, preferred_element_type=WIDE
    ).astype(jnp.int32)
    own_ranks = jnp.sum(jnp.where(own_hot, ranks[:seq_count], 0), axis=0)
    targets = own_docs * capacity + own_ranks
    slots = jnp.arange(seq_count * capacity, dtype=jnp.int32)
    send_hot = (targets[None, :] == slots[:, None]).astype(LOW)
    sent = jnp.dot(send_hot, states, preferred_element_type=WIDE).astype(LOW)
    arrived = lax.all_to_all(sent, "seq", split_axis=0, concat_axis=0, tiled=True)
    arrival = jnp.where(mine, ranks[seq_count:], capacity)
    hit = arrival[:, None, :] == jnp.arange(capacity, dtype=jnp.int32)[None, :, None]
    slot_position = jnp.max(jnp.where(hit, positions_all[:, None, :], -1), axis=2).reshape(-1)
    place_hot = (
        slot_position[None, :] == jnp.arange(row_count, dtype=jnp.int32)[:, None]
    ).astype(LOW)
    return jnp.dot(place_hot, arrived, preferred_element_type=WIDE).astype(LOW)


def shards(
    queries, states, state_doc, state_pos, lengths, offsets, key_weight, value_weight, context_grad
):
    seq_count = lax.axis_size("seq")
    tp_count = lax.axis_size("tp")
    device = lax.axis_index("seq")
    part = lax.axis_index("tp")
    major, minor = line_shape(seq_count)
    z, x = device // minor, device % minor
    row_count = states.shape[0]
    feature_count = key_weight.shape[0]
    slice_width = feature_count // seq_count
    quarter = row_count // tp_count
    head_count = key_weight.shape[1] // HEAD_DIM
    group_count = 4
    heads = head_count // group_count
    width = heads * HEAD_DIM

    def at(major_index, minor_index):
        return major_index * minor + minor_index

    def step_up(value, first, last):
        pairs = [(at(i, j), at(i + 1, j)) for i in range(first, last) for j in range(minor)]
        return lax.ppermute(value, "seq", pairs)

    def step_down(value, first, last):
        pairs = [(at(i, j), at(i - 1, j)) for i in range(first, last) for j in range(minor)]
        return lax.ppermute(value, "seq", pairs)

    def turn(value, shift):
        pairs = [(at(i, j), at(i, (j + shift) % minor)) for i in range(major) for j in range(minor)]
        return lax.ppermute(value, "seq", pairs)

    with jax.named_scope("route"):
        doc_part = route(states, state_doc, state_pos)
    with jax.named_scope("gather_states"):
        doc_states = lax.all_gather(doc_part, "tp", axis=1, tiled=True)
    own_rows = lax.dynamic_slice_in_dim(doc_states, part * quarter, quarter, 0)

    with jax.named_scope("line_states"):
        blocks = own_rows.reshape(quarter, major, minor * slice_width).transpose(1, 0, 2)
        groups = [[at(i, j) for i in range(major)] for j in range(minor)]
        blocks = lax.all_to_all(
            blocks, "seq", split_axis=0, concat_axis=0, axis_index_groups=groups, tiled=True
        )
        order = (z - jnp.arange(major)) % major
        blocks = jnp.take(blocks, order, axis=0)
        line_states = lax.all_gather(blocks, "tp", axis=0, tiled=False)
        line_states = line_states.reshape(tp_count * major * quarter, minor * slice_width)

    with jax.named_scope("side_states"):
        sides = own_rows.reshape(quarter, major, minor, slice_width)
        gathered = []
        for shift in range(1, minor):
            wanted = lax.dynamic_index_in_dim(sides, (x + shift) % minor, 2, keepdims=False)
            got = turn(wanted.transpose(1, 0, 2), shift)
            gathered.append(lax.all_gather(got, "tp", axis=1, tiled=True))
        own_side = lax.dynamic_index_in_dim(
            doc_states.reshape(row_count, major, minor, slice_width), x, 2, keepdims=False
        ).transpose(1, 0, 2)
        side_states = jnp.concatenate([own_side] + gathered, axis=1)

    info = jnp.stack(
        [
            lax.dynamic_index_in_dim(lengths, device, 0, keepdims=False),
            lax.dynamic_index_in_dim(offsets, device, 0, keepdims=False),
        ]
    )
    query_grads, rows_grads = [], []
    for group in range(group_count):
        with jax.named_scope(f"attend_{group}"):
            columns = slice(group * width, (group + 1) * width)
            key_rows = jnp.dot(doc_states, key_weight[:, columns], preferred_element_type=WIDE)
            value_rows = jnp.dot(doc_states, value_weight[:, columns], preferred_element_type=WIDE)
            query_grad, rows_grad = attend(
                info, queries, key_rows.astype(LOW), value_rows.astype(LOW), context_grad,
                group * heads, heads,
            )
            query_grads.append(query_grad)
            rows_grads.append(rows_grad)

    even = [rows_grads[0], rows_grads[2]]
    odd = [rows_grads[1], rows_grads[3]]
    rows_up, rows_down = [[g] for g in even], [[g] for g in even]
    odd_rows = [None, None]
    sums_up, sums_down = [None, None], [None, None]

    def side_product(index, dest):
        return down_dot(
            lax.dynamic_index_in_dim(side_states, dest, 0, keepdims=False), odd_rows[index]
        )

    for step in range(major):
        distance = major - step
        for index in range(2):
            with jax.named_scope(f"rows_{step}_{index}"):
                if step < major - 1:
                    rows_up[index].append(step_up(rows_up[index][-1], step, major - 1))
                    rows_down[index].append(step_down(rows_down[index][-1], 1, major - step))
            with jax.named_scope(f"sums_{step}_{index}"):
                if step == 0:
                    odd_rows[index] = jnp.concatenate(
                        [odd[index]] + [turn(odd[index], shift) for shift in range(1, minor)], axis=0
                    )
                else:
                    if 2 * distance >= major:
                        up_product = down_product = side_product(
                            index, jnp.where(z + distance < major, z + distance, jnp.maximum(z - distance, 0))
                        )
                    else:
                        up_product = side_product(index, jnp.minimum(z + distance, major - 1))
                        down_product = side_product(index, jnp.maximum(z - distance, 0))
                    if sums_up[index] is not None:
                        up_product = up_product + sums_up[index].astype(WIDE)
                        down_product = down_product + sums_down[index].astype(WIDE)
                    sums_up[index] = step_up(up_product.astype(LOW), 0, major - distance)
                    sums_down[index] = step_down(down_product.astype(LOW), distance, major)

    results = [None] * group_count
    for index in range(2):
        with jax.named_scope(f"even_{index}"):
            pieces = [even[index]]
            for j in range(1, major):
                pieces.append(jnp.where(z >= j, rows_up[index][j], rows_down[index][major - j]))
            line_rows = jnp.concatenate(
                [piece.reshape(tp_count, 1, quarter, 2 * width) for piece in pieces], axis=1
            ).reshape(tp_count * major * quarter, 2 * width)

            def line_product(dest):
                chosen = lax.dynamic_slice_in_dim(line_states, dest * slice_width, slice_width, 1)
                return down_dot(chosen, line_rows)

            arrivals = [
                turn(line_product((x + shift) % minor).astype(LOW), shift) for shift in range(1, minor)
            ]
            total = line_product(x)
            for arrival in arrivals:
                total = total + arrival.astype(WIDE)
            results[2 * index] = total.astype(LOW)
        with jax.named_scope(f"odd_{index}"):
            total = side_product(index, z)
            total = total + sums_up[index].astype(WIDE) + sums_down[index].astype(WIDE)
            results[2 * index + 1] = total.astype(LOW)

    return (
        jnp.concatenate(query_grads, axis=1),
        jnp.concatenate([result[:, :width] for result in results], axis=1),
        jnp.concatenate([result[:, width:] for result in results], axis=1),
    )


def solution(mesh):
    in_specs = (
        P("seq", "tp"),
        P("seq", "tp"),
        P(),
        P(),
        P(),
        P(),
        P(None, "tp"),
        P(None, "tp"),
        P("seq", "tp"),
    )
    out_specs = (P("seq", "tp"), P("seq", "tp"), P("seq", "tp"))
    return jax.shard_map(shards, mesh=mesh, in_specs=in_specs, out_specs=out_specs, check_vma=False)
```

```python
import jax
import jax.numpy as jnp
from jax import lax
from jax.experimental import pallas as pl
from jax.experimental.pallas import tpu as pltpu
from jax.sharding import PartitionSpec as P

HEAD_DIM = 128
VMEM_LIMIT = 60 * 1024 * 1024


def cost(rank):
    return pl.CostEstimate(flops=0, bytes_accessed=rank * 2**19, transcendentals=0)
LOW = jnp.bfloat16
WIDE = jnp.float32


def attend_kernel(
    info_ref, states_ref, key_weight_ref, value_weight_ref, query_ref, grad_ref, query_grad_ref, rows_grad_ref
):
    length = info_ref[0]
    offset = info_ref[1]
    scale = HEAD_DIM ** (-0.5)
    across = (((1,), (1,)), ((), ()))
    down = (((0,), (0,)), ((), ()))
    query_count, block = query_ref.shape
    state_count = states_ref.shape[0]
    key_rows = jnp.dot(states_ref[...], key_weight_ref[...], preferred_element_type=WIDE).astype(LOW)
    value_rows = jnp.dot(states_ref[...], value_weight_ref[...], preferred_element_type=WIDE).astype(LOW)
    position = lax.broadcasted_iota(jnp.int32, (query_count, state_count), 1)
    limit = jnp.minimum(
        lax.broadcasted_iota(jnp.int32, (query_count, 1), 0) + (offset + 1), length
    )
    visible = position < limit
    for head in range(block // HEAD_DIM):
        columns = slice(head * HEAD_DIM, (head + 1) * HEAD_DIM)
        query, grad = query_ref[:, columns], grad_ref[:, columns]
        key, value = key_rows[:, columns], value_rows[:, columns]
        scores = lax.dot_general(query, key, across, preferred_element_type=WIDE) * scale
        scores = jnp.where(visible, scores, -1e30)
        weights = jnp.exp(scores - jnp.max(scores, axis=-1, keepdims=True))
        probs = weights * (1.0 / jnp.sum(weights, axis=-1, keepdims=True))
        probs_low = probs.astype(LOW)
        context = jnp.dot(probs_low, value, preferred_element_type=WIDE)
        delta = jnp.sum(grad.astype(WIDE) * context, axis=-1, keepdims=True)
        prob_grad = lax.dot_general(grad, value, across, preferred_element_type=WIDE)
        score_grad = (probs * (prob_grad - delta) * scale).astype(LOW)
        query_grad_ref[:, columns] = jnp.dot(score_grad, key, preferred_element_type=WIDE).astype(LOW)
        key_grad = lax.dot_general(score_grad, query, down, preferred_element_type=WIDE)
        value_grad = lax.dot_general(probs_low, grad, down, preferred_element_type=WIDE)
        rows_grad_ref[:, columns] = key_grad.astype(LOW)
        value_columns = slice(block + head * HEAD_DIM, block + (head + 1) * HEAD_DIM)
        rows_grad_ref[:, value_columns] = value_grad.astype(LOW)


def attend(rank, info, doc_states, key_weight, value_weight, queries, grads, first, heads):
    query_count = queries.shape[0]
    state_count, feature_count = doc_states.shape
    pair = 2 if heads % 2 == 0 and first % 2 == 0 else 1
    block = pair * HEAD_DIM
    width = heads * HEAD_DIM
    return pl.pallas_call(
        attend_kernel,
        grid=(heads // pair,),
        in_specs=[
            pl.BlockSpec(memory_space=pltpu.SMEM),
            pl.BlockSpec((state_count, feature_count), lambda h: (0, 0), pipeline_mode=pl.Buffered(1)),
            pl.BlockSpec((feature_count, block), lambda h: (0, first // pair + h)),
            pl.BlockSpec((feature_count, block), lambda h: (0, first // pair + h)),
            pl.BlockSpec((query_count, block), lambda h: (0, first // pair + h)),
            pl.BlockSpec((query_count, block), lambda h: (0, first // pair + h)),
        ],
        out_specs=[
            pl.BlockSpec((query_count, block), lambda h: (0, h)),
            pl.BlockSpec((state_count, 2 * block), lambda h: (0, h)),
        ],
        out_shape=[
            jax.ShapeDtypeStruct((query_count, width), LOW),
            jax.ShapeDtypeStruct((state_count, 2 * width), LOW),
        ],
        compiler_params=pltpu.CompilerParams(vmem_limit_bytes=40 * 1024 * 1024),
        cost_estimate=cost(rank),
    )(info, doc_states, key_weight, value_weight, queries, grads)


def products(rank, scalars, z_slot, count, terms, rows, slice_width, block):
    columns = terms[0][2][0][0].shape[1]
    arrays, specs = [], []
    for left, place, rights, _ in terms:
        for k in range(count):
            arrays.append(left)
            specs.append(pl.BlockSpec((rows, slice_width), lambda c, s, k=k, place=place: place(k, s)))
        for right, row in rights:
            arrays.append(right)
            specs.append(pl.BlockSpec((rows, block), lambda c, s, row=row: (row, c)))

    def body(scalar_ref, *refs):
        refs = list(refs)
        totals = [None] * count
        for _, _, rights, limit in terms:
            lefts = [refs.pop(0) for _ in range(count)]
            right = refs.pop(0)[...]
            if len(rights) == 2:
                right = jnp.where(scalar_ref[z_slot] >= limit, right, refs.pop(0)[...])
            for k in range(count):
                product = lax.dot_general(
                    lefts[k][...], right, (((0,), (0,)), ((), ())), preferred_element_type=WIDE
                )
                totals[k] = product if totals[k] is None else totals[k] + product
        for k in range(count):
            refs[k][...] = totals[k].astype(LOW)

    return pl.pallas_call(
        body,
        grid_spec=pltpu.PrefetchScalarGridSpec(
            num_scalar_prefetch=1,
            grid=(columns // block,),
            in_specs=specs,
            out_specs=[pl.BlockSpec((slice_width, block), lambda c, s: (0, c))] * count,
        ),
        out_shape=[jax.ShapeDtypeStruct((slice_width, columns), LOW)] * count,
        compiler_params=pltpu.CompilerParams(vmem_limit_bytes=VMEM_LIMIT),
        cost_estimate=cost(rank),
    )(scalars, *arrays)


def add_arrivals(rank, scalars, bases, arrivals, block):
    slice_width, columns = bases[0].shape
    count = len(bases)

    def body(scalar_ref, *refs):
        for base_ref, ref, out_ref in zip(refs[:count], refs[count:], refs[2 * count :]):
            out_ref[...] = (base_ref[...].astype(WIDE) + ref[...].astype(WIDE)).astype(LOW)

    flat = pl.BlockSpec((slice_width, block), lambda c, s: (0, c))
    return pl.pallas_call(
        body,
        grid_spec=pltpu.PrefetchScalarGridSpec(
            num_scalar_prefetch=1,
            grid=(columns // block,),
            in_specs=[flat] * (2 * count),
            out_specs=[flat] * count,
        ),
        out_shape=[jax.ShapeDtypeStruct((slice_width, columns), LOW)] * count,
        compiler_params=pltpu.CompilerParams(vmem_limit_bytes=VMEM_LIMIT),
        cost_estimate=cost(rank),
    )(scalars, *bases, *arrivals)


def choose(rank, scalars, z_slot, limit, up, down, block):
    rows, columns = up.shape

    def body(scalar_ref, up_ref, down_ref, out_ref):
        out_ref[...] = jnp.where(scalar_ref[z_slot] >= limit, up_ref[...], down_ref[...])

    spec = pl.BlockSpec((rows, block), lambda c, s: (0, c))
    return pl.pallas_call(
        body,
        grid_spec=pltpu.PrefetchScalarGridSpec(
            num_scalar_prefetch=1, grid=(columns // block,), in_specs=[spec] * 2, out_specs=spec
        ),
        out_shape=jax.ShapeDtypeStruct(up.shape, LOW),
        compiler_params=pltpu.CompilerParams(vmem_limit_bytes=VMEM_LIMIT),
        cost_estimate=cost(rank),
    )(scalars, up, down)


def finish(rank, scalars, addends, results, shape, first, block):
    slice_width, columns = addends[0].shape
    arrays = list(addends)
    specs = [pl.BlockSpec((slice_width, block), lambda c, s: (0, c))] * len(addends)
    aliases = {}
    if results is not None:
        aliases = {1 + len(arrays): 0, 2 + len(arrays): 1}
        arrays += list(results)
        specs += [pl.BlockSpec(memory_space=pl.ANY)] * 2

    def body(scalar_ref, *refs):
        total = refs[0][...].astype(WIDE)
        for ref in refs[1 : len(addends)]:
            total = total + ref[...].astype(WIDE)
        half = total.shape[1] // 2
        refs[-2][...] = total[:, :half].astype(LOW)
        refs[-1][...] = total[:, half:].astype(LOW)

    return pl.pallas_call(
        body,
        grid_spec=pltpu.PrefetchScalarGridSpec(
            num_scalar_prefetch=1,
            grid=(columns // block,),
            in_specs=specs,
            out_specs=[pl.BlockSpec((slice_width, block // 2), lambda c, s: (0, first + c))] * 2,
        ),
        out_shape=[jax.ShapeDtypeStruct(shape, LOW)] * 2,
        input_output_aliases=aliases,
        compiler_params=pltpu.CompilerParams(vmem_limit_bytes=VMEM_LIMIT),
        cost_estimate=cost(rank),
    )(scalars, *arrays)


def line_shape(seq_count):
    minor = 1
    while (2 * minor) ** 2 <= seq_count and seq_count % (2 * minor) == 0:
        minor *= 2
    return seq_count // minor, minor


def route(states, state_doc, state_pos):
    seq_count = lax.axis_size("seq")
    device = lax.axis_index("seq")
    row_count = states.shape[0]
    capacity = 3 * row_count // (4 * seq_count) + row_count // 16
    docs_all = state_doc.reshape(seq_count, row_count)
    positions_all = state_pos.reshape(seq_count, row_count)
    before = (
        lax.broadcasted_iota(jnp.int32, (row_count, row_count), 0)
        < lax.broadcasted_iota(jnp.int32, (row_count, row_count), 1)
    ).astype(LOW)
    own_docs = lax.dynamic_index_in_dim(docs_all, device, 0, keepdims=False)
    doc_ids = jnp.arange(seq_count, dtype=jnp.int32)
    own_hot = own_docs[None, :] == doc_ids[:, None]
    mine = docs_all == device
    ranks = jnp.dot(
        jnp.concatenate([own_hot, mine], axis=0).astype(LOW), before, preferred_element_type=WIDE
    ).astype(jnp.int32)
    own_ranks = jnp.sum(jnp.where(own_hot, ranks[:seq_count], 0), axis=0)
    targets = own_docs * capacity + own_ranks
    slots = jnp.arange(seq_count * capacity, dtype=jnp.int32)
    send_hot = (targets[None, :] == slots[:, None]).astype(LOW)
    sent = jnp.dot(send_hot, states, preferred_element_type=WIDE).astype(LOW)
    arrived = lax.all_to_all(sent, "seq", split_axis=0, concat_axis=0, tiled=True)
    arrival = jnp.where(mine, ranks[seq_count:], capacity)
    hit = arrival[:, None, :] == jnp.arange(capacity, dtype=jnp.int32)[None, :, None]
    slot_position = jnp.max(jnp.where(hit, positions_all[:, None, :], -1), axis=2).reshape(-1)
    place_hot = (
        slot_position[None, :] == jnp.arange(row_count, dtype=jnp.int32)[:, None]
    ).astype(LOW)
    return jnp.dot(place_hot, arrived, preferred_element_type=WIDE).astype(LOW)


def shards(
    queries, states, state_doc, state_pos, lengths, offsets, key_weight, value_weight, context_grad
):
    seq_count = lax.axis_size("seq")
    tp_count = lax.axis_size("tp")
    device = lax.axis_index("seq")
    part = lax.axis_index("tp")
    major, minor = line_shape(seq_count)
    z, x = device // minor, device % minor
    row_count = states.shape[0]
    feature_count = key_weight.shape[0]
    slice_width = feature_count // seq_count
    quarter = row_count // tp_count
    head_count = key_weight.shape[1] // HEAD_DIM
    group_count = 4
    heads = head_count // group_count
    width = heads * HEAD_DIM

    def at(major_index, minor_index):
        return major_index * minor + minor_index

    def step_up(value, first, last):
        pairs = [(at(i, j), at(i + 1, j)) for i in range(first, last) for j in range(minor)]
        return lax.ppermute(value, "seq", pairs)

    def step_down(value, first, last):
        pairs = [(at(i, j), at(i - 1, j)) for i in range(first, last) for j in range(minor)]
        return lax.ppermute(value, "seq", pairs)

    def turn(value, shift):
        pairs = [(at(i, j), at(i, (j + shift) % minor)) for i in range(major) for j in range(minor)]
        return lax.ppermute(value, "seq", pairs)

    with jax.named_scope("route"):
        doc_part = route(states, state_doc, state_pos)

    with jax.named_scope("line_states"):
        ratio = tp_count // major
        slots = [i for i in range(0, major, 2)] + [i for i in range(1, major, 2)]
        pairs = []
        for i in range(major):
            for j in range(minor):
                for t in range(tp_count):
                    to = t // ratio
                    slot = slots.index((to - i) % major) * ratio + t % ratio
                    pairs.append((at(i, j) * tp_count + t, at(to, j) * tp_count + slot))
        moved = lax.ppermute(doc_part, ("seq", "tp"), pairs)
    side_parts = []
    if ratio == 1:
        with jax.named_scope("side_states"):
            for shift in range(1, minor):
                wanted = lax.dynamic_slice_in_dim(
                    doc_part, ((x + shift) % minor) * slice_width, slice_width, 1
                )
                side_parts.append(turn(wanted, shift))
    with jax.named_scope("gather_states"):
        doc_states = lax.all_gather(doc_part, "tp", axis=1, tiled=True)
    doc_states, moved, *side_parts = lax.optimization_barrier((doc_states, moved, *side_parts))
    with jax.named_scope("side_states"):
        if ratio == 1:
            side_states = [
                lax.all_gather(piece, "tp", axis=0, tiled=True) for piece in side_parts
            ]
        else:
            own_rows = lax.dynamic_slice_in_dim(doc_states, part * quarter, quarter, 0)
            side_states = []
            for shift in range(1, minor):
                wanted = jnp.concatenate(
                    [
                        lax.dynamic_slice_in_dim(
                            own_rows, at(i, (x + shift) % minor) * slice_width, slice_width, 1
                        )
                        for i in range(major)
                    ],
                    axis=1,
                )
                side_states.append(lax.all_gather(turn(wanted, shift), "tp", axis=0, tiled=True))
    with jax.named_scope("line_states"):
        line_states = lax.all_gather(moved, "tp", axis=0, tiled=True)
        if ratio > 1:
            line_states = line_states.reshape(major, ratio, row_count, -1).transpose(0, 2, 1, 3)
        line_states = line_states.reshape(major * row_count, minor * slice_width)

    def nearest(distance):
        return jnp.where(z + distance < major, z + distance, jnp.maximum(z - distance, 0))

    def dests_from(step):
        found = []
        for distance in range(major - step, 0, -1):
            if 2 * distance >= major:
                found.append(nearest(distance))
            else:
                found += [jnp.minimum(z + distance, major - 1), jnp.maximum(z - distance, 0)]
        return found + [z]

    first_dests, later_dests = [nearest(major - 1)], dests_from(2)
    side_dests = [(x + shift) % minor for shift in range(1, minor)] + [x]
    table = [
        lax.dynamic_index_in_dim(lengths, device, 0, keepdims=False),
        lax.dynamic_index_in_dim(offsets, device, 0, keepdims=False),
        z,
    ]
    z_slot = 2
    first_slot = len(table)
    table += [at(dest, x) for dest in first_dests] + first_dests
    later_slot = len(table)
    table += [at(dest, x) for dest in later_dests] + later_dests
    side_slot = len(table)
    table += side_dests
    table = jnp.stack([jnp.asarray(value, jnp.int32) for value in table])

    latest, pending, rank = None, [], 0

    def scalars():
        nonlocal rank
        rank += 1
        others = [] if latest is None else [latest]
        others += pending
        pending.clear()
        return lax.optimization_barrier((table, *others))[0]

    query_grads = [None] * group_count

    def attend_group(group):
        nonlocal latest
        with jax.named_scope(f"attend_{group}"):
            info = scalars()
            query_grads[group], latest = attend(
                rank, info, doc_states, key_weight, value_weight, queries, context_grad,
                group * heads, heads,
            )
            return latest

    even, odd = [None, None], [None, None]
    rows_up, rows_down = [[], []], [[], []]
    odd_rows = [None, None]
    sums_up, sums_down = [None, None], [None, None]
    side_own = [None, None]
    side_ahead, line_ahead, even_sums = [None, None], [None, None], [None, None]
    block = 4 * HEAD_DIM if heads % 2 == 0 else 2 * HEAD_DIM

    def send_first(index):
        with jax.named_scope(f"rows_0_{index}"):
            rows_up[index] = [(even[index], 0), (step_up(even[index], 0, major - 1), 0)]
            rows_down[index] = [(even[index], 0), (step_down(even[index], 1, major), 0)]

    def first_arrives(index):
        pending.extend([rows_up[index][1][0], rows_down[index][1][0]])

    def send_rows(step, index, before):
        nonlocal latest
        with jax.named_scope(f"rows_{step}_{index}"):
            up, down = rows_up[index][step][0], rows_down[index][step][0]
            others = [rows_up[before[1]][before[0] + 1][0], rows_down[before[1]][before[0] + 1][0]]
            if 2 * step < major:
                up, down = lax.optimization_barrier((up, down, latest, *others))[:2]
                up, down = step_up(up, step, major - 1), step_down(down, 1, major - step)
            else:
                pending.extend(others)
                info = scalars()
                latest = both = choose(rank, info, z_slot, step, up, down, block)
                pairs = [(at(i, j), at(i + 1, j)) for i in range(step, major - 1) for j in range(minor)]
                pairs += [(at(i, j), at(i - 1, j)) for i in range(1, major - step) for j in range(minor)]
                up = down = lax.ppermute(both, "seq", pairs)
            rows_up[index].append((up, 0))
            rows_down[index].append((down, 0))

    def send_odd(index):
        with jax.named_scope(f"side_rows_{index}"):
            odd_rows[index] = [odd[index]] + [turn(odd[index], shift) for shift in range(1, minor)]

    def side_products(index, slot, total, skip, count, free=False):
        nonlocal latest
        terms = [(doc_states, lambda k, s: (0, s[slot + skip + k]), [(odd_rows[index][0], 0)], None)]
        for states_of, rows_of in zip(side_states, odd_rows[index][1:]):
            if ratio == 1:
                place = lambda k, s: (s[slot + total + skip + k], 0)
            else:
                place = lambda k, s: (0, s[slot + total + skip + k])
            terms.append((states_of, place, [(rows_of, 0)], None))
        info = scalars()
        found = products(0 if free else rank, info, z_slot, count, terms, row_count, slice_width, block)
        latest = found[-1]
        return found

    def send_sums(step, index):
        nonlocal latest
        distance = major - step
        up_pairs = [(at(i, j), at(i + 1, j)) for i in range(major - distance) for j in range(minor)]
        down_pairs = [(at(i, j), at(i - 1, j)) for i in range(distance, major) for j in range(minor)]
        with jax.named_scope(f"sums_{step}_{index}"):
            if step == 1:
                up = down = side_products(index, first_slot, 1, 0, 1)[0]
            else:
                place = len(later_dests) - len(dests_from(step))
                info = scalars()
                up, down = sums_up[index], sums_down[index]
                if up is down and 2 * distance >= major:
                    (up,) = add_arrivals(rank, info, [side_ahead[index][place]], [up], block)
                    down = up
                else:
                    bases = [side_ahead[index][place], side_ahead[index][place + (2 * distance < major)]]
                    up, down = add_arrivals(rank, info, bases, [up, down], block)
                latest = down
            if 2 * distance > major + 1 and up is down:
                sums_up[index] = sums_down[index] = lax.ppermute(up, "seq", up_pairs + down_pairs)
            else:
                sums_up[index] = lax.ppermute(up, "seq", up_pairs)
                sums_down[index] = lax.ppermute(down, "seq", down_pairs)

    def products_ahead(index):
        with jax.named_scope(f"side_ahead_{index}"):
            count = len(later_dests)
            if count > 1:
                side_ahead[index] = side_products(index, later_slot, count, 0, count - 1, True)

    def own_product(index, *awaited):
        with jax.named_scope(f"side_own_{index}"):
            pending.extend(awaited)
            count = len(later_dests)
            side_own[index] = side_products(index, later_slot, count, count - 1, 1)[0]

    def send_even(index):
        nonlocal latest
        with jax.named_scope(f"even_{index}"):
            terms = []
            for j in range(major):
                rights = [(even[index], 0)] if j == 0 else [rows_up[index][j], rows_down[index][major - j]]
                place = lambda k, s, slot=slots.index(j): (slot, s[side_slot + k])
                terms.append((line_states, place, rights, j if j else None))
            info = scalars()
            *sent, line_ahead[index] = products(
                rank, info, z_slot, minor, terms, row_count, slice_width, block
            )
            latest = line_ahead[index]
            even_sums[index] = [turn(value, shift) for shift, value in enumerate(sent, 1)]

    results = None
    steps = 2 * width // block

    def finish_group(addends, group):
        nonlocal latest, results
        with jax.named_scope(f"finish_{group}"):
            info = scalars()
            results = finish(
                rank, info, addends, results, (slice_width, key_weight.shape[1]), group * steps, block
            )
            latest = results[0]

    even[0] = attend_group(0)
    send_first(0)
    odd[0] = attend_group(2)
    send_odd(0)
    even[1] = attend_group(1)
    send_first(1)
    first_arrives(0)
    odd[1] = attend_group(3)
    send_odd(1)
    send_sums(1, 0)
    if major > 2:
        send_rows(1, 0, (0, 1))
    products_ahead(0)
    send_sums(1, 1)
    for step in range(2, major):
        if step > 2:
            send_rows(step - 1, 1, (step - 1, 0))
        send_sums(step, 0)
        if step == 2:
            send_rows(1, 1, (1, 0))
            products_ahead(1)
            own_product(1, sums_up[1], sums_down[1])
        if step < major - 1:
            send_rows(step, 0, (step - 1, 1))
        else:
            send_even(0)
        send_sums(step, 1)
        if step == 2:
            own_product(0, sums_up[0], sums_down[0])
    if major == 2:
        own_product(1)
        own_product(0)
        send_even(0)
    send_even(1)
    finish_group([side_own[0], sums_up[0], sums_down[0]], 2)
    finish_group([line_ahead[0], *even_sums[0]], 0)
    finish_group([side_own[1], sums_up[1], sums_down[1]], 3)
    finish_group([line_ahead[1], *even_sums[1]], 1)

    return (jnp.concatenate(query_grads, axis=1), *results)


def solution(mesh):
    in_specs = (
        P("seq", "tp"),
        P("seq", "tp"),
        P(),
        P(),
        P(),
        P(),
        P(None, "tp"),
        P(None, "tp"),
        P("seq", "tp"),
    )
    out_specs = (P("seq", "tp"), P("seq", "tp"), P("seq", "tp"))
    return jax.shard_map(shards, mesh=mesh, in_specs=in_specs, out_specs=out_specs, check_vma=False)
```

```python
import jax
import jax.numpy as jnp
from jax import lax
from jax.experimental import pallas as pl
from jax.experimental.pallas import tpu as pltpu
from jax.sharding import PartitionSpec as P

HEAD_DIM = 128
VMEM_LIMIT = 60 * 1024 * 1024
SMALL_LIMIT = 16 * 1024 * 1024


def cost(rank):
    return pl.CostEstimate(flops=0, bytes_accessed=rank * 2**19, transcendentals=0)
LOW = jnp.bfloat16
WIDE = jnp.float32


def attend_kernel(pieces, info_ref, *refs):
    states_refs, key_refs, value_refs = refs[:pieces], refs[pieces : 2 * pieces], refs[2 * pieces : 3 * pieces]
    query_ref, grad_ref, query_grad_ref, rows_grad_ref = refs[3 * pieces :]
    length = info_ref[0]
    offset = info_ref[1]
    scale = HEAD_DIM ** (-0.5)
    across = (((1,), (1,)), ((), ()))
    down = (((0,), (0,)), ((), ()))
    query_count, block = query_ref.shape
    state_count = states_refs[0].shape[0]

    def project(weight_refs):
        total = None
        for states_ref, weight_ref in zip(states_refs, weight_refs):
            weight = weight_ref[...].reshape(-1, block)
            product = jnp.dot(states_ref[...], weight, preferred_element_type=WIDE)
            total = product if total is None else total + product
        return total.astype(LOW)

    key_rows, value_rows = project(key_refs), project(value_refs)
    position = lax.broadcasted_iota(jnp.int32, (query_count, state_count), 1)
    limit = jnp.minimum(
        lax.broadcasted_iota(jnp.int32, (query_count, 1), 0) + (offset + 1), length
    )
    visible = position < limit
    for head in range(block // HEAD_DIM):
        columns = slice(head * HEAD_DIM, (head + 1) * HEAD_DIM)
        query, grad = query_ref[:, columns], grad_ref[:, columns]
        key, value = key_rows[:, columns], value_rows[:, columns]
        scores = lax.dot_general(query, key, across, preferred_element_type=WIDE) * scale
        scores = jnp.where(visible, scores, -1e30)
        weights = jnp.exp(scores - jnp.max(scores, axis=-1, keepdims=True))
        probs = weights * (1.0 / jnp.sum(weights, axis=-1, keepdims=True))
        probs_low = probs.astype(LOW)
        context = jnp.dot(probs_low, value, preferred_element_type=WIDE)
        delta = jnp.sum(grad.astype(WIDE) * context, axis=-1, keepdims=True)
        prob_grad = lax.dot_general(grad, value, across, preferred_element_type=WIDE)
        score_grad = (probs * (prob_grad - delta) * scale).astype(LOW)
        query_grad_ref[:, columns] = jnp.dot(score_grad, key, preferred_element_type=WIDE).astype(LOW)
        key_grad = lax.dot_general(score_grad, query, down, preferred_element_type=WIDE)
        value_grad = lax.dot_general(probs_low, grad, down, preferred_element_type=WIDE)
        rows_grad_ref[:, columns] = key_grad.astype(LOW)
        value_columns = slice(block + head * HEAD_DIM, block + (head + 1) * HEAD_DIM)
        rows_grad_ref[:, value_columns] = value_grad.astype(LOW)


def attend(rank, info, doc_states, key_weight, value_weight, queries, grads, first, heads):
    query_count = queries.shape[0]
    pieces = len(doc_states)
    state_count, feature_count = doc_states[0].shape
    part_count, _, part_features, _ = key_weight.shape
    pair = 2 if heads % 2 == 0 and first % 2 == 0 else 1
    block = pair * HEAD_DIM
    width = heads * HEAD_DIM
    weight_specs = [
        pl.BlockSpec(
            (part_count, 1, part_features, block), lambda h, piece=piece: (0, piece, 0, first // pair + h)
        )
        for piece in range(pieces)
    ]
    states_spec = pl.BlockSpec(
        (state_count, feature_count), lambda h: (0, 0), pipeline_mode=pl.Buffered(1)
    )
    return pl.pallas_call(
        lambda *refs: attend_kernel(pieces, *refs),
        grid=(heads // pair,),
        in_specs=[
            pl.BlockSpec(memory_space=pltpu.SMEM),
            *[states_spec] * pieces,
            *weight_specs,
            *weight_specs,
            pl.BlockSpec((query_count, block), lambda h: (0, first // pair + h)),
            pl.BlockSpec((query_count, block), lambda h: (0, first // pair + h)),
        ],
        out_specs=[
            pl.BlockSpec((query_count, block), lambda h: (0, h)),
            pl.BlockSpec((state_count, 2 * block), lambda h: (0, h)),
        ],
        out_shape=[
            jax.ShapeDtypeStruct((query_count, width), LOW),
            jax.ShapeDtypeStruct((state_count, 2 * width), LOW),
        ],
        compiler_params=pltpu.CompilerParams(vmem_limit_bytes=40 * 1024 * 1024),
        cost_estimate=cost(rank),
    )(info, *doc_states, *[key_weight] * pieces, *[value_weight] * pieces, queries, grads)


def products(rank, scalars, z_slot, count, terms, rows, slice_width, block):
    columns = terms[0][2][0][0].shape[1]
    arrays, specs = [], []
    for left, place, rights, _ in terms:
        for k in range(count):
            arrays.append(left)
            specs.append(pl.BlockSpec((rows, slice_width), lambda c, s, k=k, place=place: place(k, s)))
        for right, row in rights:
            arrays.append(right)
            specs.append(pl.BlockSpec((rows, block), lambda c, s, row=row: (row, c)))

    def body(scalar_ref, *refs):
        refs = list(refs)
        totals = [None] * count
        for _, _, rights, limit in terms:
            lefts = [refs.pop(0) for _ in range(count)]
            right = refs.pop(0)[...]
            if len(rights) == 2:
                right = jnp.where(scalar_ref[z_slot] >= limit, right, refs.pop(0)[...])
            for k in range(count):
                product = lax.dot_general(
                    lefts[k][...], right, (((0,), (0,)), ((), ())), preferred_element_type=WIDE
                )
                totals[k] = product if totals[k] is None else totals[k] + product
        for k in range(count):
            refs[k][...] = totals[k].astype(LOW)

    return pl.pallas_call(
        body,
        grid_spec=pltpu.PrefetchScalarGridSpec(
            num_scalar_prefetch=1,
            grid=(columns // block,),
            in_specs=specs,
            out_specs=[pl.BlockSpec((slice_width, block), lambda c, s: (0, c))] * count,
        ),
        out_shape=[jax.ShapeDtypeStruct((slice_width, columns), LOW)] * count,
        compiler_params=pltpu.CompilerParams(vmem_limit_bytes=VMEM_LIMIT),
        cost_estimate=cost(rank),
    )(scalars, *arrays)


def add_arrivals(rank, scalars, bases, arrivals, block):
    slice_width, columns = bases[0].shape
    count = len(bases)

    def body(scalar_ref, *refs):
        for base_ref, ref, out_ref in zip(refs[:count], refs[count:], refs[2 * count :]):
            out_ref[...] = (base_ref[...].astype(WIDE) + ref[...].astype(WIDE)).astype(LOW)

    flat = pl.BlockSpec((slice_width, block), lambda c, s: (0, c))
    return pl.pallas_call(
        body,
        grid_spec=pltpu.PrefetchScalarGridSpec(
            num_scalar_prefetch=1,
            grid=(columns // block,),
            in_specs=[flat] * (2 * count),
            out_specs=[flat] * count,
        ),
        out_shape=[jax.ShapeDtypeStruct((slice_width, columns), LOW)] * count,
        compiler_params=pltpu.CompilerParams(vmem_limit_bytes=SMALL_LIMIT),
        cost_estimate=cost(rank),
    )(scalars, *bases, *arrivals)


def choose(rank, scalars, z_slot, limit, up, down, block):
    rows, columns = up.shape

    def body(scalar_ref, up_ref, down_ref, out_ref):
        out_ref[...] = jnp.where(scalar_ref[z_slot] >= limit, up_ref[...], down_ref[...])

    spec = pl.BlockSpec((rows, block), lambda c, s: (0, c))
    return pl.pallas_call(
        body,
        grid_spec=pltpu.PrefetchScalarGridSpec(
            num_scalar_prefetch=1, grid=(columns // block,), in_specs=[spec] * 2, out_specs=spec
        ),
        out_shape=jax.ShapeDtypeStruct(up.shape, LOW),
        compiler_params=pltpu.CompilerParams(vmem_limit_bytes=SMALL_LIMIT),
        cost_estimate=cost(rank),
    )(scalars, up, down)


def finish(rank, scalars, addends, results, shape, first, block):
    slice_width, columns = addends[0].shape
    arrays = list(addends)
    specs = [pl.BlockSpec((slice_width, block), lambda c, s: (0, c))] * len(addends)
    aliases = {}
    if results is not None:
        aliases = {1 + len(arrays): 0, 2 + len(arrays): 1}
        arrays += list(results)
        specs += [pl.BlockSpec(memory_space=pl.ANY)] * 2

    def body(scalar_ref, *refs):
        total = refs[0][...].astype(WIDE)
        for ref in refs[1 : len(addends)]:
            total = total + ref[...].astype(WIDE)
        half = total.shape[1] // 2
        refs[-2][...] = total[:, :half].astype(LOW)
        refs[-1][...] = total[:, half:].astype(LOW)

    return pl.pallas_call(
        body,
        grid_spec=pltpu.PrefetchScalarGridSpec(
            num_scalar_prefetch=1,
            grid=(columns // block,),
            in_specs=specs,
            out_specs=[pl.BlockSpec((slice_width, block // 2), lambda c, s: (0, first + c))] * 2,
        ),
        out_shape=[jax.ShapeDtypeStruct(shape, LOW)] * 2,
        input_output_aliases=aliases,
        compiler_params=pltpu.CompilerParams(vmem_limit_bytes=SMALL_LIMIT),
        cost_estimate=cost(rank),
    )(scalars, *arrays)


def line_shape(seq_count):
    minor = 1
    while (2 * minor) ** 2 <= seq_count and seq_count % (2 * minor) == 0:
        minor *= 2
    return seq_count // minor, minor


def route(states, state_doc, state_pos, pieces, table):
    seq_count = lax.axis_size("seq")
    device = lax.axis_index("seq")
    row_count = states.shape[0]
    capacity = 3 * row_count // (4 * seq_count) + row_count // 16
    docs_all = state_doc.reshape(seq_count, row_count)
    positions_all = state_pos.reshape(seq_count, row_count)
    before = (
        lax.broadcasted_iota(jnp.int32, (row_count, row_count), 0)
        < lax.broadcasted_iota(jnp.int32, (row_count, row_count), 1)
    ).astype(LOW)
    own_docs = lax.dynamic_index_in_dim(docs_all, device, 0, keepdims=False)
    doc_ids = jnp.arange(seq_count, dtype=jnp.int32)
    own_hot = own_docs[None, :] == doc_ids[:, None]
    mine = docs_all == device
    ranks = jnp.dot(
        jnp.concatenate([own_hot, mine], axis=0).astype(LOW), before, preferred_element_type=WIDE
    ).astype(jnp.int32)
    own_ranks = jnp.sum(jnp.where(own_hot, ranks[:seq_count], 0), axis=0)
    targets = own_docs * capacity + own_ranks
    slots = jnp.arange(seq_count * capacity, dtype=jnp.int32)
    send_hot = (targets[None, :] == slots[:, None]).astype(LOW)
    piece_width = states.shape[1] // pieces
    arrived = []
    for piece in range(pieces):
        columns = states[:, piece * piece_width : (piece + 1) * piece_width]
        sent = jnp.dot(send_hot, columns, preferred_element_type=WIDE).astype(LOW)
        arrived.append(lax.all_to_all(sent, "seq", split_axis=0, concat_axis=0, tiled=True))
    arrival = jnp.where(mine, ranks[seq_count:], capacity)
    hit = arrival[:, None, :] == jnp.arange(capacity, dtype=jnp.int32)[None, :, None]
    slot_position = jnp.max(jnp.where(hit, positions_all[:, None, :], -1), axis=2).reshape(-1)
    place_hot = (
        slot_position[None, :] == jnp.arange(row_count, dtype=jnp.int32)[:, None]
    ).astype(LOW)
    arrived[0], table = lax.optimization_barrier((arrived[0], table))
    return [jnp.dot(place_hot, piece, preferred_element_type=WIDE).astype(LOW) for piece in arrived], table


def shards(
    queries, states, state_doc, state_pos, lengths, offsets, key_weight, value_weight, context_grad
):
    seq_count = lax.axis_size("seq")
    tp_count = lax.axis_size("tp")
    device = lax.axis_index("seq")
    part = lax.axis_index("tp")
    major, minor = line_shape(seq_count)
    z, x = device // minor, device % minor
    row_count = states.shape[0]
    feature_count = key_weight.shape[0]
    slice_width = feature_count // seq_count
    quarter = row_count // tp_count
    head_count = key_weight.shape[1] // HEAD_DIM
    group_count = 4
    heads = head_count // group_count
    width = heads * HEAD_DIM

    def at(major_index, minor_index):
        return major_index * minor + minor_index

    def step_up(value, first, last):
        pairs = [(at(i, j), at(i + 1, j)) for i in range(first, last) for j in range(minor)]
        return lax.ppermute(value, "seq", pairs)

    def step_down(value, first, last):
        pairs = [(at(i, j), at(i - 1, j)) for i in range(first, last) for j in range(minor)]
        return lax.ppermute(value, "seq", pairs)

    def turn(value, shift):
        pairs = [(at(i, j), at(i, (j + shift) % minor)) for i in range(major) for j in range(minor)]
        return lax.ppermute(value, "seq", pairs)

    pieces = seq_count // tp_count
    if minor % pieces or pieces > 2:
        pieces = 1
    def nearest(distance):
        return jnp.where(z + distance < major, z + distance, jnp.maximum(z - distance, 0))

    def dests_from(step):
        found = []
        for distance in range(major - step, 0, -1):
            if 2 * distance >= major:
                found.append(nearest(distance))
            else:
                found += [jnp.minimum(z + distance, major - 1), jnp.maximum(z - distance, 0)]
        return found + [z]

    first_dests, later_dests = [nearest(major - 1)], dests_from(2)
    side_dests = [(x + shift) % minor for shift in range(1, minor)] + [x]
    table = [
        lax.dynamic_index_in_dim(lengths, device, 0, keepdims=False),
        lax.dynamic_index_in_dim(offsets, device, 0, keepdims=False),
        z,
    ]
    z_slot = 2
    first_slot = len(table)
    table += [at(dest, x) // pieces for dest in first_dests] + first_dests
    later_slot = len(table)
    table += [at(dest, x) // pieces for dest in later_dests] + later_dests
    side_slot = len(table)
    table += side_dests
    table = jnp.stack([jnp.asarray(value, jnp.int32) for value in table])

    with jax.named_scope("route"):
        doc_pieces, table = route(states, state_doc, state_pos, pieces, table)
        doc_part = jnp.concatenate(doc_pieces, axis=1) if pieces > 1 else doc_pieces[0]

    ratio = tp_count // major
    slots = list(range(1, major, 2)) + list(range(2, major, 2)) + [0]
    piece_rows = row_count // ratio
    distance = jnp.asarray(slots, jnp.int32)[part // ratio]

    def send_line(states_of, piece):
        with jax.named_scope(f"line_states_{piece}"):
            rows = lax.dynamic_slice_in_dim(states_of, part % ratio * piece_rows, piece_rows, 0)
            found = [
                lax.dynamic_slice_in_dim(
                    rows, at((z + distance) % major, j) // pieces * slice_width, slice_width, 1
                )
                for j in range(piece, minor, pieces)
            ]
            rows = jnp.concatenate(found, axis=1) if len(found) > 1 else found[0]
            pairs = []
            for i in range(major):
                for j in range(minor):
                    for t in range(tp_count):
                        if slots[t // ratio]:
                            to = at((i + slots[t // ratio]) % major, j)
                            pairs.append((at(i, j) * tp_count + t, to * tp_count + t))
            return rows, lax.ppermute(rows, ("seq", "tp"), pairs)

    side_parts = []
    if ratio == 1:
        with jax.named_scope("side_states"):
            for shift in range(1, minor):
                wanted = lax.dynamic_slice_in_dim(
                    doc_part, ((x + shift) % minor) * slice_width, slice_width, 1
                )
                side_parts.append(turn(wanted, shift))
    with jax.named_scope("gather_states"):
        doc_states = [lax.all_gather(piece, "tp", axis=1, tiled=True) for piece in doc_pieces]
    found = [send_line(doc_states[piece], piece) for piece in range(pieces - 1)]
    joined = lax.optimization_barrier((*doc_states, *[got for _, got in found], *side_parts))
    doc_states, side_parts = list(joined[:pieces]), joined[2 * pieces - 1 :]
    found = [(rows, got) for (rows, _), got in zip(found, joined[pieces : 2 * pieces - 1])]
    found.append(send_line(doc_states[-1], pieces - 1))

    def gather_line(after):
        with jax.named_scope("line_states"):
            arrived = lax.optimization_barrier((*[got for _, got in found], after))[:-1]
            pieces_found = [jnp.where(distance == 0, rows, got) for (rows, _), got in zip(found, arrived)]
            if 1 < pieces < minor:
                rows = [rows.reshape(piece_rows, minor // pieces, 1, slice_width) for rows in pieces_found]
                rows = jnp.concatenate(rows, axis=2).reshape(piece_rows, minor * slice_width)
            else:
                rows = jnp.concatenate(pieces_found, axis=1)
            return lax.all_gather(rows, "tp", axis=0, tiled=True)

    def piece_of(minor_index):
        if pieces == 1:
            return doc_states[0]
        return jnp.where(minor_index % 2 == 1, doc_states[1], doc_states[0])

    with jax.named_scope("side_states"):
        if ratio == 1:
            side_states = [
                lax.all_gather(piece, "tp", axis=0, tiled=True) for piece in side_parts
            ]
        else:
            side_states = []
            for shift in range(1, minor):
                own_rows = lax.dynamic_slice_in_dim(piece_of(x + shift), part * quarter, quarter, 0)
                wanted = jnp.concatenate(
                    [
                        lax.dynamic_slice_in_dim(
                            own_rows, at(i, (x + shift) % minor) // pieces * slice_width, slice_width, 1
                        )
                        for i in range(major)
                    ],
                    axis=1,
                )
                side_states.append(lax.all_gather(turn(wanted, shift), "tp", axis=0, tiled=True))
        own_states = piece_of(x)
    latest, pending, rank = None, [], 0

    def scalars():
        nonlocal rank
        rank += 1
        others = [] if latest is None else [latest]
        others += pending
        pending.clear()
        return lax.optimization_barrier((table, *others))[0]

    weight_shape = (tp_count, pieces, feature_count // (tp_count * pieces), key_weight.shape[1])
    key_parts, value_parts = key_weight.reshape(weight_shape), value_weight.reshape(weight_shape)
    query_grads = [None] * group_count

    def attend_group(group):
        nonlocal latest
        with jax.named_scope(f"attend_{group}"):
            info = scalars()
            query_grads[group], latest = attend(
                rank, info, doc_states, key_parts, value_parts, queries, context_grad,
                group * heads, heads,
            )
            return latest

    even, odd = [None, None], [None, None]
    rows_up, rows_down = [[], []], [[], []]
    odd_rows = [None, None]
    sums_up, sums_down = [None, None], [None, None]
    side_own = [None, None]
    side_ahead, line_ahead, even_sums = [None, None], [None, None], [None, None]
    block = 4 * HEAD_DIM if heads % 2 == 0 else 2 * HEAD_DIM

    def send_first(index):
        with jax.named_scope(f"rows_0_{index}"):
            rows_up[index] = [(even[index], 0), (step_up(even[index], 0, major - 1), 0)]
            rows_down[index] = [(even[index], 0), (step_down(even[index], 1, major), 0)]

    def first_arrives(index):
        pending.extend([rows_up[index][1][0], rows_down[index][1][0]])

    def send_rows(step, index, before):
        nonlocal latest
        with jax.named_scope(f"rows_{step}_{index}"):
            up, down = rows_up[index][step][0], rows_down[index][step][0]
            others = [rows_up[before[1]][before[0] + 1][0], rows_down[before[1]][before[0] + 1][0]]
            if 2 * step < major:
                up, down = lax.optimization_barrier((up, down, latest, *others))[:2]
                up, down = step_up(up, step, major - 1), step_down(down, 1, major - step)
            else:
                pending.extend(others)
                info = scalars()
                latest = both = choose(rank, info, z_slot, step, up, down, block)
                pairs = [(at(i, j), at(i + 1, j)) for i in range(step, major - 1) for j in range(minor)]
                pairs += [(at(i, j), at(i - 1, j)) for i in range(1, major - step) for j in range(minor)]
                up = down = lax.ppermute(both, "seq", pairs)
            rows_up[index].append((up, 0))
            rows_down[index].append((down, 0))

    def send_odd(index):
        with jax.named_scope(f"side_rows_{index}"):
            odd_rows[index] = [odd[index]] + [turn(odd[index], shift) for shift in range(1, minor)]

    def side_products(index, slot, total, skip, count, free=False):
        nonlocal latest
        terms = [(own_states, lambda k, s: (0, s[slot + skip + k]), [(odd_rows[index][0], 0)], None)]
        for states_of, rows_of in zip(side_states, odd_rows[index][1:]):
            if ratio == 1:
                place = lambda k, s: (s[slot + total + skip + k], 0)
            else:
                place = lambda k, s: (0, s[slot + total + skip + k])
            terms.append((states_of, place, [(rows_of, 0)], None))
        info = scalars()
        found = products(0 if free else rank, info, z_slot, count, terms, row_count, slice_width, block)
        latest = found[-1]
        return found

    def send_sums(step, index):
        nonlocal latest
        distance = major - step
        up_pairs = [(at(i, j), at(i + 1, j)) for i in range(major - distance) for j in range(minor)]
        down_pairs = [(at(i, j), at(i - 1, j)) for i in range(distance, major) for j in range(minor)]
        with jax.named_scope(f"sums_{step}_{index}"):
            if step == 1:
                up = down = side_products(index, first_slot, 1, 0, 1)[0]
            else:
                place = len(later_dests) - len(dests_from(step))
                info = scalars()
                up, down = sums_up[index], sums_down[index]
                if up is down and 2 * distance >= major:
                    (up,) = add_arrivals(rank, info, [side_ahead[index][place]], [up], block)
                    down = up
                else:
                    bases = [side_ahead[index][place], side_ahead[index][place + (2 * distance < major)]]
                    up, down = add_arrivals(rank, info, bases, [up, down], block)
                latest = down
            if 2 * distance > major + 1 and up is down:
                sums_up[index] = sums_down[index] = lax.ppermute(up, "seq", up_pairs + down_pairs)
            else:
                sums_up[index] = lax.ppermute(up, "seq", up_pairs)
                sums_down[index] = lax.ppermute(down, "seq", down_pairs)

    def products_ahead(index):
        with jax.named_scope(f"side_ahead_{index}"):
            count = len(later_dests)
            if count > 1:
                side_ahead[index] = side_products(index, later_slot, count, 0, count - 1, True)

    def own_product(index, *awaited):
        with jax.named_scope(f"side_own_{index}"):
            pending.extend(awaited)
            count = len(later_dests)
            side_own[index] = side_products(index, later_slot, count, count - 1, 1)[0]

    def send_even(index):
        nonlocal latest
        with jax.named_scope(f"even_{index}"):
            terms = []
            for j in range(major):
                rights = [(even[index], 0)] if j == 0 else [rows_up[index][j], rows_down[index][major - j]]
                place = lambda k, s, slot=slots.index(j): (slot, s[side_slot + k])
                terms.append((line_states, place, rights, j if j else None))
            info = scalars()
            *sent, line_ahead[index] = products(
                rank, info, z_slot, minor, terms, row_count, slice_width, block
            )
            latest = line_ahead[index]
            even_sums[index] = [turn(value, shift) for shift, value in enumerate(sent, 1)]

    results = None
    steps = 2 * width // block

    def finish_group(addends, group):
        nonlocal latest, results
        with jax.named_scope(f"finish_{group}"):
            info = scalars()
            results = finish(
                rank, info, addends, results, (slice_width, key_weight.shape[1]), group * steps, block
            )
            latest = results[0]

    even[0] = attend_group(0)
    send_first(0)
    line_states = gather_line(latest)
    odd[0] = attend_group(2)
    send_odd(0)
    even[1] = attend_group(1)
    send_first(1)
    first_arrives(0)
    odd[1] = attend_group(3)
    send_odd(1)
    send_sums(1, 0)
    if major > 2:
        send_rows(1, 0, (0, 1))
    products_ahead(0)
    send_sums(1, 1)
    for step in range(2, major):
        if step > 2:
            send_rows(step - 1, 1, (step - 1, 0))
        send_sums(step, 0)
        if step == 2:
            send_rows(1, 1, (1, 0))
            products_ahead(1)
            own_product(1, sums_up[1], sums_down[1])
        if step < major - 1:
            send_rows(step, 0, (step - 1, 1))
        else:
            send_even(0)
        send_sums(step, 1)
        if step == 2:
            own_product(0, sums_up[0], sums_down[0])
    if major == 2:
        own_product(1)
        own_product(0)
        send_even(0)
    send_even(1)
    finish_group([side_own[0], sums_up[0], sums_down[0]], 2)
    finish_group([line_ahead[0], *even_sums[0]], 0)
    finish_group([side_own[1], sums_up[1], sums_down[1]], 3)
    finish_group([line_ahead[1], *even_sums[1]], 1)

    return (jnp.concatenate(query_grads, axis=1), *results)


def solution(mesh):
    in_specs = (
        P("seq", "tp"),
        P("seq", "tp"),
        P(),
        P(),
        P(),
        P(),
        P(None, "tp"),
        P(None, "tp"),
        P("seq", "tp"),
    )
    out_specs = (P("seq", "tp"), P("seq", "tp"), P("seq", "tp"))
    return jax.shard_map(shards, mesh=mesh, in_specs=in_specs, out_specs=out_specs, check_vma=False)
```

```python
import jax
import jax.numpy as jnp
from jax import lax
from jax.experimental import pallas as pl
from jax.experimental.pallas import tpu as pltpu
from jax.sharding import PartitionSpec as P

HEAD_DIM = 128
VMEM_LIMIT = 60 * 1024 * 1024
SMALL_LIMIT = 16 * 1024 * 1024


def cost(rank):
    return pl.CostEstimate(flops=0, bytes_accessed=rank * 2**19, transcendentals=0)
LOG2_E = 1.4426950408889634
LOW = jnp.bfloat16
WIDE = jnp.float32


def attend_kernel(pieces, info_ref, *refs):
    states_refs, key_refs, value_refs = refs[:pieces], refs[pieces : 2 * pieces], refs[2 * pieces : 3 * pieces]
    query_ref, grad_ref, query_grad_ref, rows_grad_ref = refs[3 * pieces :]
    length = info_ref[0]
    offset = info_ref[1]
    scale = HEAD_DIM ** (-0.5)
    across = (((1,), (1,)), ((), ()))
    down = (((0,), (0,)), ((), ()))
    query_count, block = query_ref.shape
    state_count = states_refs[0].shape[0]

    def project(weight_refs):
        total = None
        for states_ref, weight_ref in zip(states_refs, weight_refs):
            weight = weight_ref[...].reshape(-1, block)
            product = jnp.dot(states_ref[...], weight, preferred_element_type=WIDE)
            total = product if total is None else total + product
        return total.astype(LOW)

    key_rows, value_rows = project(key_refs), project(value_refs)
    position = lax.broadcasted_iota(jnp.int32, (query_count, state_count), 1)
    limit = jnp.minimum(
        lax.broadcasted_iota(jnp.int32, (query_count, 1), 0) + (offset + 1), length
    )
    visible = position < limit
    heads = range(block // HEAD_DIM)
    columns = [slice(head * HEAD_DIM, (head + 1) * HEAD_DIM) for head in heads]
    query = [query_ref[:, part] for part in columns]
    grad = [grad_ref[:, part] for part in columns]
    key = [key_rows[:, part] for part in columns]
    value = [value_rows[:, part] for part in columns]

    def dots(left, right, dims):
        return [
            lax.dot_general(left[head], right[head], dims, preferred_element_type=WIDE) for head in heads
        ]

    scores = [jnp.where(visible, one, -1e30) for one in dots(query, key, across)]
    prob_grad = dots(grad, value, across)
    weights = [
        jnp.exp2((one - jnp.max(one, axis=-1, keepdims=True)) * (scale * LOG2_E)) for one in scores
    ]
    probs = [one * (1.0 / jnp.sum(one, axis=-1, keepdims=True)) for one in weights]
    probs_low = [one.astype(LOW) for one in probs]
    delta = [
        jnp.sum(probs_low[head].astype(WIDE) * prob_grad[head], axis=-1, keepdims=True) for head in heads
    ]
    score_grad = [
        (probs[head] * (prob_grad[head] - delta[head]) * scale).astype(LOW) for head in heads
    ]
    query_grads = dots(score_grad, key, (((1,), (0,)), ((), ())))
    key_grads = dots(query, score_grad, down)
    value_grads = dots(grad, probs_low, down)
    for head in heads:
        query_grad_ref[:, columns[head]] = query_grads[head].astype(LOW)
        rows_grad_ref[:, columns[head]] = key_grads[head].T.astype(LOW)
        value_columns = slice(block + head * HEAD_DIM, block + (head + 1) * HEAD_DIM)
        rows_grad_ref[:, value_columns] = value_grads[head].T.astype(LOW)


def attend(rank, info, doc_states, key_weight, value_weight, queries, grads, first, heads):
    query_count = queries.shape[0]
    pieces = len(doc_states)
    state_count, feature_count = doc_states[0].shape
    part_count, _, part_features, _ = key_weight.shape
    pair = 2 if heads % 2 == 0 and first % 2 == 0 else 1
    block = pair * HEAD_DIM
    width = heads * HEAD_DIM
    weight_specs = [
        pl.BlockSpec(
            (part_count, 1, part_features, block), lambda h, piece=piece: (0, piece, 0, first // pair + h)
        )
        for piece in range(pieces)
    ]
    states_spec = pl.BlockSpec(
        (state_count, feature_count), lambda h: (0, 0), pipeline_mode=pl.Buffered(1)
    )
    return pl.pallas_call(
        lambda *refs: attend_kernel(pieces, *refs),
        grid=(heads // pair,),
        in_specs=[
            pl.BlockSpec(memory_space=pltpu.SMEM),
            *[states_spec] * pieces,
            *weight_specs,
            *weight_specs,
            pl.BlockSpec((query_count, block), lambda h: (0, first // pair + h)),
            pl.BlockSpec((query_count, block), lambda h: (0, first // pair + h)),
        ],
        out_specs=[
            pl.BlockSpec((query_count, block), lambda h: (0, h)),
            pl.BlockSpec((state_count, 2 * block), lambda h: (0, h)),
        ],
        out_shape=[
            jax.ShapeDtypeStruct((query_count, width), LOW),
            jax.ShapeDtypeStruct((state_count, 2 * width), LOW),
        ],
        compiler_params=pltpu.CompilerParams(vmem_limit_bytes=40 * 1024 * 1024),
        cost_estimate=cost(rank),
    )(info, *doc_states, *[key_weight] * pieces, *[value_weight] * pieces, queries, grads)


def products(rank, scalars, z_slot, count, terms, rows, slice_width, block):
    columns = terms[0][2][0][0].shape[1]
    arrays, specs = [], []
    for left, place, rights, _ in terms:
        for k in range(count):
            arrays.append(left)
            specs.append(pl.BlockSpec((rows, slice_width), lambda c, s, k=k, place=place: place(k, s)))
        for right, row in rights:
            arrays.append(right)
            specs.append(pl.BlockSpec((rows, block), lambda c, s, row=row: (row, c)))

    def body(scalar_ref, *refs):
        refs = list(refs)
        totals = [None] * count
        for _, _, rights, limit in terms:
            lefts = [refs.pop(0) for _ in range(count)]
            right = refs.pop(0)[...]
            if len(rights) == 2:
                right = jnp.where(scalar_ref[z_slot] >= limit, right, refs.pop(0)[...])
            for k in range(count):
                product = lax.dot_general(
                    lefts[k][...], right, (((0,), (0,)), ((), ())), preferred_element_type=WIDE
                )
                totals[k] = product if totals[k] is None else totals[k] + product
        for k in range(count):
            refs[k][...] = totals[k].astype(LOW)

    return pl.pallas_call(
        body,
        grid_spec=pltpu.PrefetchScalarGridSpec(
            num_scalar_prefetch=1,
            grid=(columns // block,),
            in_specs=specs,
            out_specs=[pl.BlockSpec((slice_width, block), lambda c, s: (0, c))] * count,
        ),
        out_shape=[jax.ShapeDtypeStruct((slice_width, columns), LOW)] * count,
        compiler_params=pltpu.CompilerParams(vmem_limit_bytes=VMEM_LIMIT),
        cost_estimate=cost(rank),
    )(scalars, *arrays)


def add_arrivals(rank, scalars, bases, arrivals, block):
    slice_width, columns = bases[0].shape
    count = len(bases)

    def body(scalar_ref, *refs):
        for base_ref, ref, out_ref in zip(refs[:count], refs[count:], refs[2 * count :]):
            out_ref[...] = (base_ref[...].astype(WIDE) + ref[...].astype(WIDE)).astype(LOW)

    flat = pl.BlockSpec((slice_width, block), lambda c, s: (0, c))
    return pl.pallas_call(
        body,
        grid_spec=pltpu.PrefetchScalarGridSpec(
            num_scalar_prefetch=1,
            grid=(columns // block,),
            in_specs=[flat] * (2 * count),
            out_specs=[flat] * count,
        ),
        out_shape=[jax.ShapeDtypeStruct((slice_width, columns), LOW)] * count,
        compiler_params=pltpu.CompilerParams(vmem_limit_bytes=SMALL_LIMIT),
        cost_estimate=cost(rank),
    )(scalars, *bases, *arrivals)


def choose(rank, scalars, z_slot, limit, up, down, block):
    rows, columns = up.shape

    def body(scalar_ref, up_ref, down_ref, out_ref):
        out_ref[...] = jnp.where(scalar_ref[z_slot] >= limit, up_ref[...], down_ref[...])

    spec = pl.BlockSpec((rows, block), lambda c, s: (0, c))
    return pl.pallas_call(
        body,
        grid_spec=pltpu.PrefetchScalarGridSpec(
            num_scalar_prefetch=1, grid=(columns // block,), in_specs=[spec] * 2, out_specs=spec
        ),
        out_shape=jax.ShapeDtypeStruct(up.shape, LOW),
        compiler_params=pltpu.CompilerParams(vmem_limit_bytes=SMALL_LIMIT),
        cost_estimate=cost(rank),
    )(scalars, up, down)


def finish(rank, scalars, addends, results, shape, first, block):
    slice_width, columns = addends[0].shape
    arrays = list(addends)
    specs = [pl.BlockSpec((slice_width, block), lambda c, s: (0, c))] * len(addends)
    aliases = {}
    if results is not None:
        aliases = {1 + len(arrays): 0, 2 + len(arrays): 1}
        arrays += list(results)
        specs += [pl.BlockSpec(memory_space=pl.ANY)] * 2

    def body(scalar_ref, *refs):
        total = refs[0][...].astype(WIDE)
        for ref in refs[1 : len(addends)]:
            total = total + ref[...].astype(WIDE)
        half = total.shape[1] // 2
        refs[-2][...] = total[:, :half].astype(LOW)
        refs[-1][...] = total[:, half:].astype(LOW)

    return pl.pallas_call(
        body,
        grid_spec=pltpu.PrefetchScalarGridSpec(
            num_scalar_prefetch=1,
            grid=(columns // block,),
            in_specs=specs,
            out_specs=[pl.BlockSpec((slice_width, block // 2), lambda c, s: (0, first + c))] * 2,
        ),
        out_shape=[jax.ShapeDtypeStruct(shape, LOW)] * 2,
        input_output_aliases=aliases,
        compiler_params=pltpu.CompilerParams(vmem_limit_bytes=SMALL_LIMIT),
        cost_estimate=cost(rank),
    )(scalars, *arrays)


def line_shape(seq_count):
    minor = 1
    while (2 * minor) ** 2 <= seq_count and seq_count % (2 * minor) == 0:
        minor *= 2
    return seq_count // minor, minor


def route(states, state_doc, state_pos, pieces, table):
    seq_count = lax.axis_size("seq")
    device = lax.axis_index("seq")
    row_count = states.shape[0]
    capacity = 3 * row_count // (4 * seq_count) + row_count // 16
    docs_all = state_doc.reshape(seq_count, row_count)
    positions_all = state_pos.reshape(seq_count, row_count)
    before = (
        lax.broadcasted_iota(jnp.int32, (row_count, row_count), 0)
        < lax.broadcasted_iota(jnp.int32, (row_count, row_count), 1)
    ).astype(LOW)
    own_docs = lax.dynamic_index_in_dim(docs_all, device, 0, keepdims=False)
    doc_ids = jnp.arange(seq_count, dtype=jnp.int32)
    own_hot = own_docs[None, :] == doc_ids[:, None]
    mine = docs_all == device
    ranks = jnp.dot(
        jnp.concatenate([own_hot, mine], axis=0).astype(LOW), before, preferred_element_type=WIDE
    ).astype(jnp.int32)
    own_ranks = jnp.sum(jnp.where(own_hot, ranks[:seq_count], 0), axis=0)
    targets = own_docs * capacity + own_ranks
    slots = jnp.arange(seq_count * capacity, dtype=jnp.int32)
    send_hot = (targets[None, :] == slots[:, None]).astype(LOW)
    piece_width = states.shape[1] // pieces
    arrived = []
    for piece in range(pieces):
        columns = states[:, piece * piece_width : (piece + 1) * piece_width]
        sent = jnp.dot(send_hot, columns, preferred_element_type=WIDE).astype(LOW)
        arrived.append(lax.all_to_all(sent, "seq", split_axis=0, concat_axis=0, tiled=True))
    arrival = jnp.where(mine, ranks[seq_count:], capacity)
    hit = arrival[:, None, :] == jnp.arange(capacity, dtype=jnp.int32)[None, :, None]
    slot_position = jnp.max(jnp.where(hit, positions_all[:, None, :], -1), axis=2).reshape(-1)
    place_hot = (
        slot_position[None, :] == jnp.arange(row_count, dtype=jnp.int32)[:, None]
    ).astype(LOW)
    arrived[0], table = lax.optimization_barrier((arrived[0], table))
    return [jnp.dot(place_hot, piece, preferred_element_type=WIDE).astype(LOW) for piece in arrived], table


def shards(
    queries, states, state_doc, state_pos, lengths, offsets, key_weight, value_weight, context_grad
):
    seq_count = lax.axis_size("seq")
    tp_count = lax.axis_size("tp")
    device = lax.axis_index("seq")
    part = lax.axis_index("tp")
    major, minor = line_shape(seq_count)
    z, x = device // minor, device % minor
    row_count = states.shape[0]
    feature_count = key_weight.shape[0]
    slice_width = feature_count // seq_count
    quarter = row_count // tp_count
    head_count = key_weight.shape[1] // HEAD_DIM
    group_count = 4
    heads = head_count // group_count
    width = heads * HEAD_DIM

    def at(major_index, minor_index):
        return major_index * minor + minor_index

    def step_up(value, first, last):
        pairs = [(at(i, j), at(i + 1, j)) for i in range(first, last) for j in range(minor)]
        return lax.ppermute(value, "seq", pairs)

    def step_down(value, first, last):
        pairs = [(at(i, j), at(i - 1, j)) for i in range(first, last) for j in range(minor)]
        return lax.ppermute(value, "seq", pairs)

    def turn(value, shift):
        pairs = [(at(i, j), at(i, (j + shift) % minor)) for i in range(major) for j in range(minor)]
        return lax.ppermute(value, "seq", pairs)

    pieces = seq_count // tp_count
    if minor % pieces or pieces > 2:
        pieces = 1
    def nearest(distance):
        return jnp.where(z + distance < major, z + distance, jnp.maximum(z - distance, 0))

    def dests_from(step):
        found = []
        for distance in range(major - step, 0, -1):
            if 2 * distance >= major:
                found.append(nearest(distance))
            else:
                found += [jnp.minimum(z + distance, major - 1), jnp.maximum(z - distance, 0)]
        return found + [z]

    first_dests, later_dests = [nearest(major - 1)], dests_from(2)
    side_dests = [(x + shift) % minor for shift in range(1, minor)] + [x]
    table = [
        lax.dynamic_index_in_dim(lengths, device, 0, keepdims=False),
        lax.dynamic_index_in_dim(offsets, device, 0, keepdims=False),
        z,
    ]
    z_slot = 2
    first_slot = len(table)
    table += [at(dest, x) // pieces for dest in first_dests] + first_dests
    later_slot = len(table)
    table += [at(dest, x) // pieces for dest in later_dests] + later_dests
    side_slot = len(table)
    table += side_dests
    table = jnp.stack([jnp.asarray(value, jnp.int32) for value in table])

    with jax.named_scope("route"):
        doc_pieces, table = route(states, state_doc, state_pos, pieces, table)
        doc_part = jnp.concatenate(doc_pieces, axis=1) if pieces > 1 else doc_pieces[0]

    ratio = tp_count // major
    slots = list(range(1, major, 2)) + list(range(2, major, 2)) + [0]
    piece_rows = row_count // ratio
    distance = jnp.asarray(slots, jnp.int32)[part // ratio]

    def send_line(states_of, piece):
        with jax.named_scope(f"line_states_{piece}"):
            rows = lax.dynamic_slice_in_dim(states_of, part % ratio * piece_rows, piece_rows, 0)
            found = [
                lax.dynamic_slice_in_dim(
                    rows, at((z + distance) % major, j) // pieces * slice_width, slice_width, 1
                )
                for j in range(piece, minor, pieces)
            ]
            rows = jnp.concatenate(found, axis=1) if len(found) > 1 else found[0]
            pairs = []
            for i in range(major):
                for j in range(minor):
                    for t in range(tp_count):
                        to = at((i + slots[t // ratio]) % major, j)
                        pairs.append((at(i, j) * tp_count + t, to * tp_count + t))
            return lax.ppermute(rows, ("seq", "tp"), pairs)

    side_parts = []
    if ratio == 1:
        with jax.named_scope("side_states"):
            for shift in range(1, minor):
                wanted = lax.dynamic_slice_in_dim(
                    doc_part, ((x + shift) % minor) * slice_width, slice_width, 1
                )
                side_parts.append(turn(wanted, shift))
    with jax.named_scope("gather_states"):
        doc_states = [lax.all_gather(piece, "tp", axis=1, tiled=True) for piece in doc_pieces]
    found = [send_line(doc_states[piece], piece) for piece in range(pieces - 1)]
    joined = lax.optimization_barrier((*doc_states, *found, *side_parts))
    doc_states, found, side_parts = (
        list(joined[:pieces]), list(joined[pieces : 2 * pieces - 1]), joined[2 * pieces - 1 :]
    )
    found.append(send_line(doc_states[-1], pieces - 1))

    def gather_line(after):
        with jax.named_scope("line_states"):
            pieces_found = lax.optimization_barrier((*found, after))[:-1]
            if 1 < pieces < minor:
                rows = [rows.reshape(piece_rows, minor // pieces, 1, slice_width) for rows in pieces_found]
                rows = jnp.concatenate(rows, axis=2).reshape(piece_rows, minor * slice_width)
            else:
                rows = jnp.concatenate(pieces_found, axis=1)
            return lax.all_gather(rows, "tp", axis=0, tiled=True)

    def piece_of(minor_index):
        if pieces == 1:
            return doc_states[0]
        return jnp.where(minor_index % 2 == 1, doc_states[1], doc_states[0])

    with jax.named_scope("side_states"):
        if ratio == 1:
            side_states = [
                lax.all_gather(piece, "tp", axis=0, tiled=True) for piece in side_parts
            ]
        else:
            side_states = []
            for shift in range(1, minor):
                own_rows = lax.dynamic_slice_in_dim(piece_of(x + shift), part * quarter, quarter, 0)
                wanted = jnp.concatenate(
                    [
                        lax.dynamic_slice_in_dim(
                            own_rows, at(i, (x + shift) % minor) // pieces * slice_width, slice_width, 1
                        )
                        for i in range(major)
                    ],
                    axis=1,
                )
                side_states.append(lax.all_gather(turn(wanted, shift), "tp", axis=0, tiled=True))
        own_states = piece_of(x)
    latest, pending, rank = None, [], 0

    def scalars():
        nonlocal rank
        rank += 1
        others = [] if latest is None else [latest]
        others += pending
        pending.clear()
        return lax.optimization_barrier((table, *others))[0]

    weight_shape = (tp_count, pieces, feature_count // (tp_count * pieces), key_weight.shape[1])
    key_parts, value_parts = key_weight.reshape(weight_shape), value_weight.reshape(weight_shape)
    query_grads = [None] * group_count

    def attend_group(group):
        nonlocal latest
        with jax.named_scope(f"attend_{group}"):
            info = scalars()
            query_grads[group], latest = attend(
                rank, info, doc_states, key_parts, value_parts, queries, context_grad,
                group * heads, heads,
            )
            return latest

    even, odd = [None, None], [None, None]
    rows_up, rows_down = [[], []], [[], []]
    odd_rows = [None, None]
    sums_up, sums_down = [None, None], [None, None]
    side_own = [None, None]
    side_ahead, line_ahead, even_sums = [None, None], [None, None], [None, None]
    block = 4 * HEAD_DIM if heads % 2 == 0 else 2 * HEAD_DIM

    def send_first(index):
        with jax.named_scope(f"rows_0_{index}"):
            rows_up[index] = [(even[index], 0), (step_up(even[index], 0, major - 1), 0)]
            rows_down[index] = [(even[index], 0), (step_down(even[index], 1, major), 0)]

    def first_arrives(index):
        pending.extend([rows_up[index][1][0], rows_down[index][1][0]])

    def send_rows(step, index, before):
        nonlocal latest
        with jax.named_scope(f"rows_{step}_{index}"):
            up, down = rows_up[index][step][0], rows_down[index][step][0]
            others = [rows_up[before[1]][before[0] + 1][0], rows_down[before[1]][before[0] + 1][0]]
            if 2 * step < major:
                up, down = lax.optimization_barrier((up, down, latest, *others))[:2]
                up, down = step_up(up, step, major - 1), step_down(down, 1, major - step)
            else:
                pending.extend(others)
                info = scalars()
                latest = both = choose(rank, info, z_slot, step, up, down, block)
                pairs = [(at(i, j), at(i + 1, j)) for i in range(step, major - 1) for j in range(minor)]
                pairs += [(at(i, j), at(i - 1, j)) for i in range(1, major - step) for j in range(minor)]
                up = down = lax.ppermute(both, "seq", pairs)
            rows_up[index].append((up, 0))
            rows_down[index].append((down, 0))

    def send_odd(index):
        with jax.named_scope(f"side_rows_{index}"):
            odd_rows[index] = [odd[index]] + [turn(odd[index], shift) for shift in range(1, minor)]

    def side_products(index, slot, total, skip, count, free=False):
        nonlocal latest
        terms = [(own_states, lambda k, s: (0, s[slot + skip + k]), [(odd_rows[index][0], 0)], None)]
        for states_of, rows_of in zip(side_states, odd_rows[index][1:]):
            if ratio == 1:
                place = lambda k, s: (s[slot + total + skip + k], 0)
            else:
                place = lambda k, s: (0, s[slot + total + skip + k])
            terms.append((states_of, place, [(rows_of, 0)], None))
        info = scalars()
        found = products(0 if free else rank, info, z_slot, count, terms, row_count, slice_width, block)
        latest = found[-1]
        return found

    def send_sums(step, index):
        nonlocal latest
        distance = major - step
        up_pairs = [(at(i, j), at(i + 1, j)) for i in range(major - distance) for j in range(minor)]
        down_pairs = [(at(i, j), at(i - 1, j)) for i in range(distance, major) for j in range(minor)]
        with jax.named_scope(f"sums_{step}_{index}"):
            if step == 1:
                up = down = side_products(index, first_slot, 1, 0, 1)[0]
            else:
                place = len(later_dests) - len(dests_from(step))
                info = scalars()
                up, down = sums_up[index], sums_down[index]
                if up is down and 2 * distance >= major:
                    (up,) = add_arrivals(rank, info, [side_ahead[index][place]], [up], block)
                    down = up
                else:
                    bases = [side_ahead[index][place], side_ahead[index][place + (2 * distance < major)]]
                    up, down = add_arrivals(rank, info, bases, [up, down], block)
                latest = down
            if 2 * distance > major + 1 and up is down:
                sums_up[index] = sums_down[index] = lax.ppermute(up, "seq", up_pairs + down_pairs)
            else:
                sums_up[index] = lax.ppermute(up, "seq", up_pairs)
                sums_down[index] = lax.ppermute(down, "seq", down_pairs)

    def products_ahead(index):
        with jax.named_scope(f"side_ahead_{index}"):
            count = len(later_dests)
            if count > 1:
                side_ahead[index] = side_products(index, later_slot, count, 0, count - 1, True)

    def own_product(index, *awaited):
        with jax.named_scope(f"side_own_{index}"):
            pending.extend(awaited)
            count = len(later_dests)
            side_own[index] = side_products(index, later_slot, count, count - 1, 1)[0]

    def send_even(index):
        nonlocal latest
        with jax.named_scope(f"even_{index}"):
            terms = []
            for j in range(major):
                rights = [(even[index], 0)] if j == 0 else [rows_up[index][j], rows_down[index][major - j]]
                place = lambda k, s, slot=slots.index(j): (slot, s[side_slot + k])
                terms.append((line_states, place, rights, j if j else None))
            info = scalars()
            *sent, line_ahead[index] = products(
                rank, info, z_slot, minor, terms, row_count, slice_width, block
            )
            latest = line_ahead[index]
            even_sums[index] = [turn(value, shift) for shift, value in enumerate(sent, 1)]

    results = None
    steps = 2 * width // block

    def finish_group(addends, group):
        nonlocal latest, results
        with jax.named_scope(f"finish_{group}"):
            info = scalars()
            results = finish(
                rank, info, addends, results, (slice_width, key_weight.shape[1]), group * steps, block
            )
            latest = results[0]

    even[0] = attend_group(0)
    send_first(0)
    line_states = gather_line(latest)
    odd[0] = attend_group(2)
    send_odd(0)
    even[1] = attend_group(1)
    send_first(1)
    first_arrives(0)
    odd[1] = attend_group(3)
    send_odd(1)
    send_sums(1, 0)
    if major > 2:
        send_rows(1, 0, (0, 1))
    products_ahead(0)
    send_sums(1, 1)
    for step in range(2, major):
        if step > 2:
            send_rows(step - 1, 1, (step - 1, 0))
        send_sums(step, 0)
        if step == 2:
            send_rows(1, 1, (1, 0))
            products_ahead(1)
            own_product(1, sums_up[1], sums_down[1])
        if step < major - 1:
            send_rows(step, 0, (step - 1, 1))
        else:
            send_even(0)
        send_sums(step, 1)
        if step == 2:
            own_product(0, sums_up[0], sums_down[0])
    if major == 2:
        own_product(1)
        own_product(0)
        send_even(0)
    send_even(1)
    finish_group([side_own[0], sums_up[0], sums_down[0]], 2)
    finish_group([line_ahead[0], *even_sums[0]], 0)
    finish_group([side_own[1], sums_up[1], sums_down[1]], 3)
    finish_group([line_ahead[1], *even_sums[1]], 1)

    return (jnp.concatenate(query_grads, axis=1), *results)


def solution(mesh):
    in_specs = (
        P("seq", "tp"),
        P("seq", "tp"),
        P(),
        P(),
        P(),
        P(),
        P(None, "tp"),
        P(None, "tp"),
        P("seq", "tp"),
    )
    out_specs = (P("seq", "tp"), P("seq", "tp"), P("seq", "tp"))
    return jax.shard_map(shards, mesh=mesh, in_specs=in_specs, out_specs=out_specs, check_vma=False)
```

```python
import jax
import jax.numpy as jnp
from jax import lax
from jax.experimental import pallas as pl
from jax.experimental.pallas import tpu as pltpu
from jax.sharding import PartitionSpec as P

HEAD_DIM = 128
VMEM_LIMIT = 60 * 1024 * 1024
SMALL_LIMIT = 16 * 1024 * 1024


def cost(rank):
    return pl.CostEstimate(flops=0, bytes_accessed=rank * 2**19, transcendentals=0)
LOG2_E = 1.4426950408889634
LOW = jnp.bfloat16
WIDE = jnp.float32


def attend_kernel(pieces, info_ref, *refs):
    states_refs, key_refs, value_refs = refs[:pieces], refs[pieces : 2 * pieces], refs[2 * pieces : 3 * pieces]
    *partial_refs, query_ref, grad_ref, query_grad_ref, rows_grad_ref = refs[3 * pieces :]
    length = info_ref[0]
    offset = info_ref[1]
    scale = HEAD_DIM ** (-0.5)
    across = (((1,), (1,)), ((), ()))
    down = (((0,), (0,)), ((), ()))
    query_count, block = query_ref.shape
    state_count = states_refs[0].shape[0]

    def project(weight_refs, place):
        total = None
        for ref in partial_refs:
            total = ref[:, place * block : (place + 1) * block]
        for states_ref, weight_ref in zip(states_refs, weight_refs):
            weight = weight_ref[...].reshape(-1, block)
            product = jnp.dot(states_ref[...], weight, preferred_element_type=WIDE)
            total = product if total is None else total + product
        return total.astype(LOW)

    key_rows, value_rows = project(key_refs, 0), project(value_refs, 1)
    position = lax.broadcasted_iota(jnp.int32, (query_count, state_count), 1)
    limit = jnp.minimum(
        lax.broadcasted_iota(jnp.int32, (query_count, 1), 0) + (offset + 1), length
    )
    visible = position < limit
    heads = range(block // HEAD_DIM)
    columns = [slice(head * HEAD_DIM, (head + 1) * HEAD_DIM) for head in heads]
    query = [query_ref[:, part] for part in columns]
    grad = [grad_ref[:, part] for part in columns]
    key = [key_rows[:, part] for part in columns]
    value = [value_rows[:, part] for part in columns]

    def dots(left, right, dims):
        return [
            lax.dot_general(left[head], right[head], dims, preferred_element_type=WIDE) for head in heads
        ]

    scores = [jnp.where(visible, one, -1e30) for one in dots(query, key, across)]
    prob_grad = dots(grad, value, across)
    weights = [
        jnp.exp2((one - jnp.max(one, axis=-1, keepdims=True)) * (scale * LOG2_E)) for one in scores
    ]
    probs = [one * (1.0 / jnp.sum(one, axis=-1, keepdims=True)) for one in weights]
    probs_low = [one.astype(LOW) for one in probs]
    delta = [
        jnp.sum(probs_low[head].astype(WIDE) * prob_grad[head], axis=-1, keepdims=True) for head in heads
    ]
    score_grad = [
        (probs[head] * (prob_grad[head] - delta[head]) * scale).astype(LOW) for head in heads
    ]
    query_grads = dots(score_grad, key, (((1,), (0,)), ((), ())))
    key_grads = dots(query, score_grad, down)
    value_grads = dots(grad, probs_low, down)
    for head in heads:
        query_grad_ref[:, columns[head]] = query_grads[head].astype(LOW)
        rows_grad_ref[:, columns[head]] = key_grads[head].T.astype(LOW)
        value_columns = slice(block + head * HEAD_DIM, block + (head + 1) * HEAD_DIM)
        rows_grad_ref[:, value_columns] = value_grads[head].T.astype(LOW)


def attend(rank, info, states, partial, key_weight, value_weight, queries, grads, first, heads):
    query_count = queries.shape[0]
    numbers = sorted(states)
    state_count, feature_count = states[numbers[0]].shape
    part_count, _, part_features, _ = key_weight.shape
    pair = 2 if heads % 2 == 0 and first % 2 == 0 else 1
    block = pair * HEAD_DIM
    width = heads * HEAD_DIM
    weight_specs = [
        pl.BlockSpec(
            (part_count, 1, part_features, block), lambda h, piece=piece: (0, piece, 0, first // pair + h)
        )
        for piece in numbers
    ]
    states_spec = pl.BlockSpec(
        (state_count, feature_count), lambda h: (0, 0), pipeline_mode=pl.Buffered(1)
    )
    pieces = len(numbers)
    weights = [key_weight] * pieces + [value_weight] * pieces
    pair_spec = pl.BlockSpec((state_count, 2 * block), lambda h: (0, h))
    partials = [] if partial is None else [partial]
    return pl.pallas_call(
        lambda *refs: attend_kernel(pieces, *refs),
        grid=(heads // pair,),
        in_specs=[
            pl.BlockSpec(memory_space=pltpu.SMEM),
            *[states_spec] * pieces,
            *weight_specs,
            *weight_specs,
            *[pair_spec] * len(partials),
            pl.BlockSpec((query_count, block), lambda h: (0, first // pair + h)),
            pl.BlockSpec((query_count, block), lambda h: (0, first // pair + h)),
        ],
        out_specs=[pl.BlockSpec((query_count, block), lambda h: (0, h)), pair_spec],
        out_shape=[
            jax.ShapeDtypeStruct((query_count, width), LOW),
            jax.ShapeDtypeStruct((state_count, 2 * width), LOW),
        ],
        compiler_params=pltpu.CompilerParams(vmem_limit_bytes=40 * 1024 * 1024),
        cost_estimate=cost(rank),
    )(info, *[states[number] for number in numbers], *weights, *partials, queries, grads)


def project_piece(states, piece, key_weight, value_weight, first, heads):
    state_count, feature_count = states.shape
    part_count, _, part_features, _ = key_weight.shape
    pair = 2 if heads % 2 == 0 and first % 2 == 0 else 1
    block = pair * HEAD_DIM
    weight_spec = pl.BlockSpec(
        (part_count, 1, part_features, block), lambda h: (0, piece, 0, first // pair + h)
    )

    def body(states_ref, key_ref, value_ref, out_ref):
        for place, ref in enumerate((key_ref, value_ref)):
            weight = ref[...].reshape(-1, block)
            out_ref[:, place * block : (place + 1) * block] = jnp.dot(
                states_ref[...], weight, preferred_element_type=WIDE
            )

    return pl.pallas_call(
        body,
        grid=(heads // pair,),
        in_specs=[
            pl.BlockSpec((state_count, feature_count), lambda h: (0, 0), pipeline_mode=pl.Buffered(1)),
            weight_spec,
            weight_spec,
        ],
        out_specs=pl.BlockSpec((state_count, 2 * block), lambda h: (0, h)),
        out_shape=jax.ShapeDtypeStruct((state_count, 2 * heads * HEAD_DIM), WIDE),
        compiler_params=pltpu.CompilerParams(vmem_limit_bytes=40 * 1024 * 1024),
        cost_estimate=pl.CostEstimate(
            flops=4 * state_count * feature_count * heads * HEAD_DIM,
            bytes_accessed=4 * feature_count * heads * HEAD_DIM,
            transcendentals=0,
        ),
    )(states, key_weight, value_weight)


def products(rank, scalars, z_slot, count, terms, rows, slice_width, block):
    columns = terms[0][2][0][0].shape[1]
    arrays, specs = [], []
    for left, place, rights, _ in terms:
        for k in range(count):
            arrays.append(left)
            specs.append(pl.BlockSpec((rows, slice_width), lambda c, s, k=k, place=place: place(k, s)))
        for right, row in rights:
            arrays.append(right)
            specs.append(pl.BlockSpec((rows, block), lambda c, s, row=row: (row, c)))

    def body(scalar_ref, *refs):
        refs = list(refs)
        totals = [None] * count
        for _, _, rights, limit in terms:
            lefts = [refs.pop(0) for _ in range(count)]
            right = refs.pop(0)[...]
            if len(rights) == 2:
                right = jnp.where(scalar_ref[z_slot] >= limit, right, refs.pop(0)[...])
            for k in range(count):
                product = lax.dot_general(
                    lefts[k][...], right, (((0,), (0,)), ((), ())), preferred_element_type=WIDE
                )
                totals[k] = product if totals[k] is None else totals[k] + product
        for k in range(count):
            refs[k][...] = totals[k].astype(LOW)

    return pl.pallas_call(
        body,
        grid_spec=pltpu.PrefetchScalarGridSpec(
            num_scalar_prefetch=1,
            grid=(columns // block,),
            in_specs=specs,
            out_specs=[pl.BlockSpec((slice_width, block), lambda c, s: (0, c))] * count,
        ),
        out_shape=[jax.ShapeDtypeStruct((slice_width, columns), LOW)] * count,
        compiler_params=pltpu.CompilerParams(vmem_limit_bytes=VMEM_LIMIT),
        cost_estimate=cost(rank),
    )(scalars, *arrays)


def add_arrivals(rank, scalars, bases, arrivals, block):
    slice_width, columns = bases[0].shape
    count = len(bases)

    def body(scalar_ref, *refs):
        for base_ref, ref, out_ref in zip(refs[:count], refs[count:], refs[2 * count :]):
            out_ref[...] = (base_ref[...].astype(WIDE) + ref[...].astype(WIDE)).astype(LOW)

    flat = pl.BlockSpec((slice_width, block), lambda c, s: (0, c))
    return pl.pallas_call(
        body,
        grid_spec=pltpu.PrefetchScalarGridSpec(
            num_scalar_prefetch=1,
            grid=(columns // block,),
            in_specs=[flat] * (2 * count),
            out_specs=[flat] * count,
        ),
        out_shape=[jax.ShapeDtypeStruct((slice_width, columns), LOW)] * count,
        compiler_params=pltpu.CompilerParams(vmem_limit_bytes=SMALL_LIMIT),
        cost_estimate=cost(rank),
    )(scalars, *bases, *arrivals)


def choose(rank, scalars, z_slot, limit, up, down, block):
    rows, columns = up.shape

    def body(scalar_ref, up_ref, down_ref, out_ref):
        out_ref[...] = jnp.where(scalar_ref[z_slot] >= limit, up_ref[...], down_ref[...])

    spec = pl.BlockSpec((rows, block), lambda c, s: (0, c))
    return pl.pallas_call(
        body,
        grid_spec=pltpu.PrefetchScalarGridSpec(
            num_scalar_prefetch=1, grid=(columns // block,), in_specs=[spec] * 2, out_specs=spec
        ),
        out_shape=jax.ShapeDtypeStruct(up.shape, LOW),
        compiler_params=pltpu.CompilerParams(vmem_limit_bytes=SMALL_LIMIT),
        cost_estimate=cost(rank),
    )(scalars, up, down)


def finish(rank, scalars, addends, results, shape, first, block):
    slice_width, columns = addends[0].shape
    arrays = list(addends)
    specs = [pl.BlockSpec((slice_width, block), lambda c, s: (0, c))] * len(addends)
    aliases = {}
    if results is not None:
        aliases = {1 + len(arrays): 0, 2 + len(arrays): 1}
        arrays += list(results)
        specs += [pl.BlockSpec(memory_space=pl.ANY)] * 2

    def body(scalar_ref, *refs):
        total = refs[0][...].astype(WIDE)
        for ref in refs[1 : len(addends)]:
            total = total + ref[...].astype(WIDE)
        half = total.shape[1] // 2
        refs[-2][...] = total[:, :half].astype(LOW)
        refs[-1][...] = total[:, half:].astype(LOW)

    return pl.pallas_call(
        body,
        grid_spec=pltpu.PrefetchScalarGridSpec(
            num_scalar_prefetch=1,
            grid=(columns // block,),
            in_specs=specs,
            out_specs=[pl.BlockSpec((slice_width, block // 2), lambda c, s: (0, first + c))] * 2,
        ),
        out_shape=[jax.ShapeDtypeStruct(shape, LOW)] * 2,
        input_output_aliases=aliases,
        compiler_params=pltpu.CompilerParams(vmem_limit_bytes=SMALL_LIMIT),
        cost_estimate=cost(rank),
    )(scalars, *arrays)


def line_shape(seq_count):
    minor = 1
    while (2 * minor) ** 2 <= seq_count and seq_count % (2 * minor) == 0:
        minor *= 2
    return seq_count // minor, minor


def route(states, state_doc, state_pos, pieces, table):
    seq_count = lax.axis_size("seq")
    device = lax.axis_index("seq")
    row_count = states.shape[0]
    capacity = 3 * row_count // (4 * seq_count) + row_count // 16
    docs_all = state_doc.reshape(seq_count, row_count)
    positions_all = state_pos.reshape(seq_count, row_count)
    before = (
        lax.broadcasted_iota(jnp.int32, (row_count, row_count), 0)
        < lax.broadcasted_iota(jnp.int32, (row_count, row_count), 1)
    ).astype(LOW)
    own_docs = lax.dynamic_index_in_dim(docs_all, device, 0, keepdims=False)
    doc_ids = jnp.arange(seq_count, dtype=jnp.int32)
    own_hot = own_docs[None, :] == doc_ids[:, None]
    mine = docs_all == device
    ranks = jnp.dot(
        jnp.concatenate([own_hot, mine], axis=0).astype(LOW), before, preferred_element_type=WIDE
    ).astype(jnp.int32)
    own_ranks = jnp.sum(jnp.where(own_hot, ranks[:seq_count], 0), axis=0)
    targets = own_docs * capacity + own_ranks
    slots = jnp.arange(seq_count * capacity, dtype=jnp.int32)
    send_hot = (targets[None, :] == slots[:, None]).astype(LOW)
    piece_width = states.shape[1] // pieces
    arrived = []
    for piece in range(pieces):
        columns = states[:, piece * piece_width : (piece + 1) * piece_width]
        sent = jnp.dot(send_hot, columns, preferred_element_type=WIDE).astype(LOW)
        arrived.append(lax.all_to_all(sent, "seq", split_axis=0, concat_axis=0, tiled=True))
    arrival = jnp.where(mine, ranks[seq_count:], capacity)
    hit = arrival[:, None, :] == jnp.arange(capacity, dtype=jnp.int32)[None, :, None]
    slot_position = jnp.max(jnp.where(hit, positions_all[:, None, :], -1), axis=2).reshape(-1)
    place_hot = (
        slot_position[None, :] == jnp.arange(row_count, dtype=jnp.int32)[:, None]
    ).astype(LOW)
    arrived[0], table = lax.optimization_barrier((arrived[0], table))
    return [jnp.dot(place_hot, piece, preferred_element_type=WIDE).astype(LOW) for piece in arrived], table


def shards(
    queries, states, state_doc, state_pos, lengths, offsets, key_weight, value_weight, context_grad
):
    seq_count = lax.axis_size("seq")
    tp_count = lax.axis_size("tp")
    device = lax.axis_index("seq")
    part = lax.axis_index("tp")
    major, minor = line_shape(seq_count)
    z, x = device // minor, device % minor
    row_count = states.shape[0]
    feature_count = key_weight.shape[0]
    slice_width = feature_count // seq_count
    quarter = row_count // tp_count
    head_count = key_weight.shape[1] // HEAD_DIM
    group_count = 4
    heads = head_count // group_count
    width = heads * HEAD_DIM

    def at(major_index, minor_index):
        return major_index * minor + minor_index

    def step_up(value, first, last):
        pairs = [(at(i, j), at(i + 1, j)) for i in range(first, last) for j in range(minor)]
        return lax.ppermute(value, "seq", pairs)

    def step_down(value, first, last):
        pairs = [(at(i, j), at(i - 1, j)) for i in range(first, last) for j in range(minor)]
        return lax.ppermute(value, "seq", pairs)

    def turn(value, shift):
        pairs = [(at(i, j), at(i, (j + shift) % minor)) for i in range(major) for j in range(minor)]
        return lax.ppermute(value, "seq", pairs)

    pieces = seq_count // tp_count
    if minor % pieces or pieces > 2:
        pieces = 1
    def nearest(distance):
        return jnp.where(z + distance < major, z + distance, jnp.maximum(z - distance, 0))

    def dests_from(step):
        found = []
        for distance in range(major - step, 0, -1):
            if 2 * distance >= major:
                found.append(nearest(distance))
            else:
                found += [jnp.minimum(z + distance, major - 1), jnp.maximum(z - distance, 0)]
        return found + [z]

    first_dests, later_dests = [nearest(major - 1)], dests_from(2)
    side_dests = [(x + shift) % minor for shift in range(1, minor)] + [x]
    table = [
        lax.dynamic_index_in_dim(lengths, device, 0, keepdims=False),
        lax.dynamic_index_in_dim(offsets, device, 0, keepdims=False),
        z,
    ]
    z_slot = 2
    first_slot = len(table)
    table += [at(dest, x) // pieces for dest in first_dests] + first_dests
    later_slot = len(table)
    table += [at(dest, x) // pieces for dest in later_dests] + later_dests
    side_slot = len(table)
    table += side_dests
    table = jnp.stack([jnp.asarray(value, jnp.int32) for value in table])

    with jax.named_scope("route"):
        doc_pieces, table = route(states, state_doc, state_pos, pieces, table)
        doc_part = jnp.concatenate(doc_pieces, axis=1) if pieces > 1 else doc_pieces[0]

    ratio = tp_count // major
    slots = list(range(1, major, 2)) + list(range(2, major, 2)) + [0]
    piece_rows = row_count // ratio
    distance = jnp.asarray(slots, jnp.int32)[part // ratio]

    def send_line(states_of, piece):
        with jax.named_scope(f"line_states_{piece}"):
            rows = lax.dynamic_slice_in_dim(states_of, part % ratio * piece_rows, piece_rows, 0)
            found = [
                lax.dynamic_slice_in_dim(
                    rows, at((z + distance) % major, j) // pieces * slice_width, slice_width, 1
                )
                for j in range(piece, minor, pieces)
            ]
            rows = jnp.concatenate(found, axis=1) if len(found) > 1 else found[0]
            pairs = []
            for i in range(major):
                for j in range(minor):
                    for t in range(tp_count):
                        to = at((i + slots[t // ratio]) % major, j)
                        pairs.append((at(i, j) * tp_count + t, to * tp_count + t))
            return lax.ppermute(rows, ("seq", "tp"), pairs)

    side_parts = []
    if ratio == 1:
        with jax.named_scope("side_states"):
            for shift in range(1, minor):
                wanted = lax.dynamic_slice_in_dim(
                    doc_part, ((x + shift) % minor) * slice_width, slice_width, 1
                )
                side_parts.append(turn(wanted, shift))
    with jax.named_scope("gather_states"):
        doc_states = [lax.all_gather(piece, "tp", axis=1, tiled=True) for piece in doc_pieces]
    weight_shape = (tp_count, pieces, feature_count // (tp_count * pieces), key_weight.shape[1])
    key_parts, value_parts = key_weight.reshape(weight_shape), value_weight.reshape(weight_shape)
    found = [send_line(doc_states[piece], piece) for piece in range(pieces - 1)]
    partials = [None] * group_count
    if pieces == 2:
        with jax.named_scope("project_first_piece"):
            for group in range(group_count - 1):
                partials[group] = project_piece(
                    doc_states[0], 0, key_parts, value_parts, group * heads, heads
                )
    early = [value for value in partials if value is not None]
    joined = list(lax.optimization_barrier((*doc_states, *found, *side_parts, *early)))
    doc_states = [joined.pop(0) for _ in doc_states]
    found = [joined.pop(0) for _ in found]
    side_parts = [joined.pop(0) for _ in side_parts]
    if early:
        partials = [*joined, None]
    all_states = dict(enumerate(doc_states))
    late_states = {pieces - 1: doc_states[-1]}
    found.append(send_line(doc_states[-1], pieces - 1))

    def gather_line(after):
        with jax.named_scope("line_states"):
            pieces_found = lax.optimization_barrier((*found, after))[:-1]
            if 1 < pieces < minor:
                rows = [rows.reshape(piece_rows, minor // pieces, 1, slice_width) for rows in pieces_found]
                rows = jnp.concatenate(rows, axis=2).reshape(piece_rows, minor * slice_width)
            else:
                rows = jnp.concatenate(pieces_found, axis=1)
            return lax.all_gather(rows, "tp", axis=0, tiled=True)

    def piece_of(minor_index):
        if pieces == 1:
            return doc_states[0]
        return jnp.where(minor_index % 2 == 1, doc_states[1], doc_states[0])

    with jax.named_scope("side_states"):
        if ratio == 1:
            side_states = [
                lax.all_gather(piece, "tp", axis=0, tiled=True) for piece in side_parts
            ]
        else:
            side_states = []
            for shift in range(1, minor):
                own_rows = lax.dynamic_slice_in_dim(piece_of(x + shift), part * quarter, quarter, 0)
                wanted = jnp.concatenate(
                    [
                        lax.dynamic_slice_in_dim(
                            own_rows, at(i, (x + shift) % minor) // pieces * slice_width, slice_width, 1
                        )
                        for i in range(major)
                    ],
                    axis=1,
                )
                side_states.append(lax.all_gather(turn(wanted, shift), "tp", axis=0, tiled=True))
        own_states = piece_of(x)
    latest, pending, rank = None, [], 0

    def scalars():
        nonlocal rank
        rank += 1
        others = [] if latest is None else [latest]
        others += pending
        pending.clear()
        return lax.optimization_barrier((table, *others))[0]

    query_grads = [None] * group_count

    def attend_group(group):
        nonlocal latest
        with jax.named_scope(f"attend_{group}"):
            info = scalars()
            query_grads[group], latest = attend(
                rank, info, all_states if partials[group] is None else late_states, partials[group],
                key_parts, value_parts, queries, context_grad,
                group * heads, heads,
            )
            return latest

    even, odd = [None, None], [None, None]
    rows_up, rows_down = [[], []], [[], []]
    odd_rows = [None, None]
    sums_up, sums_down = [None, None], [None, None]
    side_own = [None, None]
    side_ahead, line_ahead, even_sums = [None, None], [None, None], [None, None]
    block = 4 * HEAD_DIM if heads % 2 == 0 else 2 * HEAD_DIM

    def send_first(index):
        with jax.named_scope(f"rows_0_{index}"):
            rows_up[index] = [(even[index], 0), (step_up(even[index], 0, major - 1), 0)]
            rows_down[index] = [(even[index], 0), (step_down(even[index], 1, major), 0)]

    def first_arrives(index):
        pending.extend([rows_up[index][1][0], rows_down[index][1][0]])

    def send_rows(step, index, before):
        nonlocal latest
        with jax.named_scope(f"rows_{step}_{index}"):
            up, down = rows_up[index][step][0], rows_down[index][step][0]
            others = [rows_up[before[1]][before[0] + 1][0], rows_down[before[1]][before[0] + 1][0]]
            if 2 * step < major:
                up, down = lax.optimization_barrier((up, down, latest, *others))[:2]
                up, down = step_up(up, step, major - 1), step_down(down, 1, major - step)
            else:
                pending.extend(others)
                info = scalars()
                latest = both = choose(rank, info, z_slot, step, up, down, block)
                pairs = [(at(i, j), at(i + 1, j)) for i in range(step, major - 1) for j in range(minor)]
                pairs += [(at(i, j), at(i - 1, j)) for i in range(1, major - step) for j in range(minor)]
                up = down = lax.ppermute(both, "seq", pairs)
            rows_up[index].append((up, 0))
            rows_down[index].append((down, 0))

    def send_odd(index):
        with jax.named_scope(f"side_rows_{index}"):
            odd_rows[index] = [odd[index]] + [turn(odd[index], shift) for shift in range(1, minor)]

    def side_products(index, slot, total, skip, count, free=False):
        nonlocal latest
        terms = [(own_states, lambda k, s: (0, s[slot + skip + k]), [(odd_rows[index][0], 0)], None)]
        for states_of, rows_of in zip(side_states, odd_rows[index][1:]):
            if ratio == 1:
                place = lambda k, s: (s[slot + total + skip + k], 0)
            else:
                place = lambda k, s: (0, s[slot + total + skip + k])
            terms.append((states_of, place, [(rows_of, 0)], None))
        info = scalars()
        found = products(0 if free else rank, info, z_slot, count, terms, row_count, slice_width, block)
        latest = found[-1]
        return found

    def send_sums(step, index):
        nonlocal latest
        distance = major - step
        up_pairs = [(at(i, j), at(i + 1, j)) for i in range(major - distance) for j in range(minor)]
        down_pairs = [(at(i, j), at(i - 1, j)) for i in range(distance, major) for j in range(minor)]
        with jax.named_scope(f"sums_{step}_{index}"):
            if step == 1:
                up = down = side_products(index, first_slot, 1, 0, 1)[0]
            else:
                place = len(later_dests) - len(dests_from(step))
                info = scalars()
                up, down = sums_up[index], sums_down[index]
                if up is down and 2 * distance >= major:
                    (up,) = add_arrivals(rank, info, [side_ahead[index][place]], [up], block)
                    down = up
                else:
                    bases = [side_ahead[index][place], side_ahead[index][place + (2 * distance < major)]]
                    up, down = add_arrivals(rank, info, bases, [up, down], block)
                latest = down
            if 2 * distance > major + 1 and up is down:
                sums_up[index] = sums_down[index] = lax.ppermute(up, "seq", up_pairs + down_pairs)
            else:
                sums_up[index] = lax.ppermute(up, "seq", up_pairs)
                sums_down[index] = lax.ppermute(down, "seq", down_pairs)

    def products_ahead(index):
        with jax.named_scope(f"side_ahead_{index}"):
            count = len(later_dests)
            if count > 1:
                side_ahead[index] = side_products(index, later_slot, count, 0, count - 1, True)

    def own_product(index, *awaited):
        with jax.named_scope(f"side_own_{index}"):
            pending.extend(awaited)
            count = len(later_dests)
            side_own[index] = side_products(index, later_slot, count, count - 1, 1)[0]

    def send_even(index):
        nonlocal latest
        with jax.named_scope(f"even_{index}"):
            terms = []
            for j in range(major):
                rights = [(even[index], 0)] if j == 0 else [rows_up[index][j], rows_down[index][major - j]]
                place = lambda k, s, slot=slots.index(j): (slot, s[side_slot + k])
                terms.append((line_states, place, rights, j if j else None))
            info = scalars()
            *sent, line_ahead[index] = products(
                rank, info, z_slot, minor, terms, row_count, slice_width, block
            )
            latest = line_ahead[index]
            even_sums[index] = [turn(value, shift) for shift, value in enumerate(sent, 1)]

    results = None
    steps = 2 * width // block

    def finish_group(addends, group):
        nonlocal latest, results
        with jax.named_scope(f"finish_{group}"):
            info = scalars()
            results = finish(
                rank, info, addends, results, (slice_width, key_weight.shape[1]), group * steps, block
            )
            latest = results[0]

    even[0] = attend_group(0)
    send_first(0)
    line_states = gather_line(latest)
    odd[0] = attend_group(2)
    send_odd(0)
    even[1] = attend_group(1)
    send_first(1)
    first_arrives(0)
    odd[1] = attend_group(3)
    send_odd(1)
    send_sums(1, 0)
    if major > 2:
        send_rows(1, 0, (0, 1))
    products_ahead(0)
    send_sums(1, 1)
    for step in range(2, major):
        if step > 2:
            send_rows(step - 1, 1, (step - 1, 0))
        send_sums(step, 0)
        if step == 2:
            send_rows(1, 1, (1, 0))
            products_ahead(1)
            own_product(1, sums_up[1], sums_down[1])
        if step < major - 1:
            send_rows(step, 0, (step - 1, 1))
        else:
            send_even(0)
        send_sums(step, 1)
        if step == 2:
            own_product(0, sums_up[0], sums_down[0])
    if major == 2:
        own_product(1)
        own_product(0)
        send_even(0)
    send_even(1)
    finish_group([side_own[0], sums_up[0], sums_down[0]], 2)
    finish_group([line_ahead[0], *even_sums[0]], 0)
    finish_group([side_own[1], sums_up[1], sums_down[1]], 3)
    finish_group([line_ahead[1], *even_sums[1]], 1)

    return (jnp.concatenate(query_grads, axis=1), *results)


def solution(mesh):
    in_specs = (
        P("seq", "tp"),
        P("seq", "tp"),
        P(),
        P(),
        P(),
        P(),
        P(None, "tp"),
        P(None, "tp"),
        P("seq", "tp"),
    )
    out_specs = (P("seq", "tp"), P("seq", "tp"), P("seq", "tp"))
    return jax.shard_map(shards, mesh=mesh, in_specs=in_specs, out_specs=out_specs, check_vma=False)
```

```python
import jax
import jax.numpy as jnp
from jax import lax
from jax.experimental import pallas as pl
from jax.experimental.pallas import tpu as pltpu
from jax.sharding import PartitionSpec as P

HEAD_DIM = 128
VMEM_LIMIT = 40 * 1024 * 1024
SMALL_LIMIT = 16 * 1024 * 1024


def cost(rank):
    return pl.CostEstimate(flops=0, bytes_accessed=rank * 2**19, transcendentals=0)
LOG2_E = 1.4426950408889634
LOW = jnp.bfloat16
WIDE = jnp.float32


def attend_kernel(pieces, info_ref, *refs):
    states_refs, key_refs, value_refs = refs[:pieces], refs[pieces : 2 * pieces], refs[2 * pieces : 3 * pieces]
    *partial_refs, query_ref, grad_ref, query_grad_ref, rows_grad_ref = refs[3 * pieces :]
    length = info_ref[0]
    offset = info_ref[1]
    scale = HEAD_DIM ** (-0.5)
    across = (((1,), (1,)), ((), ()))
    down = (((0,), (0,)), ((), ()))
    query_count, block = query_ref.shape
    state_count = states_refs[0].shape[0]

    def project(weight_refs, place):
        total = None
        for ref in partial_refs:
            total = ref[:, place * block : (place + 1) * block]
        for states_ref, weight_ref in zip(states_refs, weight_refs):
            weight = weight_ref[...].reshape(-1, block)
            product = jnp.dot(states_ref[...], weight, preferred_element_type=WIDE)
            total = product if total is None else total + product
        return total.astype(LOW)

    key_rows, value_rows = project(key_refs, 0), project(value_refs, 1)
    position = lax.broadcasted_iota(jnp.int32, (query_count, state_count), 1)
    limit = jnp.minimum(
        lax.broadcasted_iota(jnp.int32, (query_count, 1), 0) + (offset + 1), length
    )
    visible = position < limit
    heads = range(block // HEAD_DIM)
    columns = [slice(head * HEAD_DIM, (head + 1) * HEAD_DIM) for head in heads]
    query = [query_ref[:, part] for part in columns]
    grad = [grad_ref[:, part] for part in columns]
    key = [key_rows[:, part] for part in columns]
    value = [value_rows[:, part] for part in columns]

    def dots(left, right, dims):
        return [
            lax.dot_general(left[head], right[head], dims, preferred_element_type=WIDE) for head in heads
        ]

    scores = [jnp.where(visible, one, -1e30) for one in dots(query, key, across)]
    prob_grad = dots(grad, value, across)
    weights = [
        jnp.exp2((one - jnp.max(one, axis=-1, keepdims=True)) * (scale * LOG2_E)) for one in scores
    ]
    probs = [one * (1.0 / jnp.sum(one, axis=-1, keepdims=True)) for one in weights]
    probs_low = [one.astype(LOW) for one in probs]
    delta = [
        jnp.sum(probs_low[head].astype(WIDE) * prob_grad[head], axis=-1, keepdims=True) for head in heads
    ]
    score_grad = [
        (probs[head] * (prob_grad[head] - delta[head]) * scale).astype(LOW) for head in heads
    ]
    query_grads = dots(score_grad, key, (((1,), (0,)), ((), ())))
    key_grads = dots(query, score_grad, down)
    value_grads = dots(grad, probs_low, down)
    for head in heads:
        query_grad_ref[:, columns[head]] = query_grads[head].astype(LOW)
        rows_grad_ref[:, columns[head]] = key_grads[head].T.astype(LOW)
        value_columns = slice(block + head * HEAD_DIM, block + (head + 1) * HEAD_DIM)
        rows_grad_ref[:, value_columns] = value_grads[head].T.astype(LOW)


def attend(rank, info, states, partial, key_weight, value_weight, queries, grads, first, heads):
    query_count = queries.shape[0]
    numbers = sorted(states)
    state_count, feature_count = states[numbers[0]].shape
    part_count, _, part_features, _ = key_weight.shape
    pair = 2 if heads % 2 == 0 and first % 2 == 0 else 1
    block = pair * HEAD_DIM
    width = heads * HEAD_DIM
    weight_specs = [
        pl.BlockSpec(
            (part_count, 1, part_features, block), lambda h, piece=piece: (0, piece, 0, first // pair + h)
        )
        for piece in numbers
    ]
    states_spec = pl.BlockSpec(
        (state_count, feature_count), lambda h: (0, 0), pipeline_mode=pl.Buffered(1)
    )
    pieces = len(numbers)
    weights = [key_weight] * pieces + [value_weight] * pieces
    pair_spec = pl.BlockSpec((state_count, 2 * block), lambda h: (0, h))
    partials = [] if partial is None else [partial]
    return pl.pallas_call(
        lambda *refs: attend_kernel(pieces, *refs),
        grid=(heads // pair,),
        in_specs=[
            pl.BlockSpec(memory_space=pltpu.SMEM),
            *[states_spec] * pieces,
            *weight_specs,
            *weight_specs,
            *[pair_spec] * len(partials),
            pl.BlockSpec((query_count, block), lambda h: (0, first // pair + h)),
            pl.BlockSpec((query_count, block), lambda h: (0, first // pair + h)),
        ],
        out_specs=[pl.BlockSpec((query_count, block), lambda h: (0, h)), pair_spec],
        out_shape=[
            jax.ShapeDtypeStruct((query_count, width), LOW),
            jax.ShapeDtypeStruct((state_count, 2 * width), LOW),
        ],
        compiler_params=pltpu.CompilerParams(vmem_limit_bytes=40 * 1024 * 1024),
        cost_estimate=cost(rank),
    )(info, *[states[number] for number in numbers], *weights, *partials, queries, grads)


def project_piece(states, piece, key_weight, value_weight, first, heads):
    state_count, feature_count = states.shape
    part_count, _, part_features, _ = key_weight.shape
    pair = 2 if heads % 2 == 0 and first % 2 == 0 else 1
    block = pair * HEAD_DIM
    weight_spec = pl.BlockSpec(
        (part_count, 1, part_features, block), lambda h: (0, piece, 0, first // pair + h)
    )

    def body(states_ref, key_ref, value_ref, out_ref):
        for place, ref in enumerate((key_ref, value_ref)):
            weight = ref[...].reshape(-1, block)
            out_ref[:, place * block : (place + 1) * block] = jnp.dot(
                states_ref[...], weight, preferred_element_type=WIDE
            )

    return pl.pallas_call(
        body,
        grid=(heads // pair,),
        in_specs=[
            pl.BlockSpec((state_count, feature_count), lambda h: (0, 0), pipeline_mode=pl.Buffered(1)),
            weight_spec,
            weight_spec,
        ],
        out_specs=pl.BlockSpec((state_count, 2 * block), lambda h: (0, h)),
        out_shape=jax.ShapeDtypeStruct((state_count, 2 * heads * HEAD_DIM), WIDE),
        compiler_params=pltpu.CompilerParams(vmem_limit_bytes=40 * 1024 * 1024),
        cost_estimate=pl.CostEstimate(
            flops=4 * state_count * feature_count * heads * HEAD_DIM,
            bytes_accessed=4 * feature_count * heads * HEAD_DIM,
            transcendentals=0,
        ),
    )(states, key_weight, value_weight)


def products(rank, scalars, z_slot, count, terms, rows, slice_width, block):
    columns = terms[0][2][0][0].shape[1]
    arrays, specs = [], []
    for left, place, rights, _ in terms:
        for k in range(count):
            arrays.append(left)
            specs.append(pl.BlockSpec((rows, slice_width), lambda c, s, k=k, place=place: place(k, s)))
        for right, row in rights:
            arrays.append(right)
            specs.append(pl.BlockSpec((rows, block), lambda c, s, row=row: (row, c)))

    def body(scalar_ref, *refs):
        refs = list(refs)
        totals = [None] * count
        for _, _, rights, limit in terms:
            lefts = [refs.pop(0) for _ in range(count)]
            right = refs.pop(0)[...]
            if len(rights) == 2:
                right = jnp.where(scalar_ref[z_slot] >= limit, right, refs.pop(0)[...])
            for k in range(count):
                product = lax.dot_general(
                    lefts[k][...], right, (((0,), (0,)), ((), ())), preferred_element_type=WIDE
                )
                totals[k] = product if totals[k] is None else totals[k] + product
        for k in range(count):
            refs[k][...] = totals[k].astype(LOW)

    return pl.pallas_call(
        body,
        grid_spec=pltpu.PrefetchScalarGridSpec(
            num_scalar_prefetch=1,
            grid=(columns // block,),
            in_specs=specs,
            out_specs=[pl.BlockSpec((slice_width, block), lambda c, s: (0, c))] * count,
        ),
        out_shape=[jax.ShapeDtypeStruct((slice_width, columns), LOW)] * count,
        compiler_params=pltpu.CompilerParams(vmem_limit_bytes=VMEM_LIMIT),
        cost_estimate=cost(rank),
    )(scalars, *arrays)


def add_arrivals(rank, scalars, bases, arrivals, block):
    slice_width, columns = bases[0].shape
    count = len(bases)

    def body(scalar_ref, *refs):
        for base_ref, ref, out_ref in zip(refs[:count], refs[count:], refs[2 * count :]):
            out_ref[...] = (base_ref[...].astype(WIDE) + ref[...].astype(WIDE)).astype(LOW)

    flat = pl.BlockSpec((slice_width, block), lambda c, s: (0, c))
    return pl.pallas_call(
        body,
        grid_spec=pltpu.PrefetchScalarGridSpec(
            num_scalar_prefetch=1,
            grid=(columns // block,),
            in_specs=[flat] * (2 * count),
            out_specs=[flat] * count,
        ),
        out_shape=[jax.ShapeDtypeStruct((slice_width, columns), LOW)] * count,
        compiler_params=pltpu.CompilerParams(vmem_limit_bytes=SMALL_LIMIT),
        cost_estimate=cost(rank),
    )(scalars, *bases, *arrivals)


def choose(rank, scalars, z_slot, limit, up, down, block):
    rows, columns = up.shape

    def body(scalar_ref, up_ref, down_ref, out_ref):
        out_ref[...] = jnp.where(scalar_ref[z_slot] >= limit, up_ref[...], down_ref[...])

    spec = pl.BlockSpec((rows, block), lambda c, s: (0, c))
    return pl.pallas_call(
        body,
        grid_spec=pltpu.PrefetchScalarGridSpec(
            num_scalar_prefetch=1, grid=(columns // block,), in_specs=[spec] * 2, out_specs=spec
        ),
        out_shape=jax.ShapeDtypeStruct(up.shape, LOW),
        compiler_params=pltpu.CompilerParams(vmem_limit_bytes=SMALL_LIMIT),
        cost_estimate=cost(rank),
    )(scalars, up, down)


def finish(rank, scalars, addends, results, shape, first, block):
    slice_width, columns = addends[0].shape
    arrays = list(addends)
    specs = [pl.BlockSpec((slice_width, block), lambda c, s: (0, c))] * len(addends)
    aliases = {}
    if results is not None:
        aliases = {1 + len(arrays): 0, 2 + len(arrays): 1}
        arrays += list(results)
        specs += [pl.BlockSpec(memory_space=pl.ANY)] * 2

    def body(scalar_ref, *refs):
        total = refs[0][...].astype(WIDE)
        for ref in refs[1 : len(addends)]:
            total = total + ref[...].astype(WIDE)
        half = total.shape[1] // 2
        refs[-2][...] = total[:, :half].astype(LOW)
        refs[-1][...] = total[:, half:].astype(LOW)

    return pl.pallas_call(
        body,
        grid_spec=pltpu.PrefetchScalarGridSpec(
            num_scalar_prefetch=1,
            grid=(columns // block,),
            in_specs=specs,
            out_specs=[pl.BlockSpec((slice_width, block // 2), lambda c, s: (0, first + c))] * 2,
        ),
        out_shape=[jax.ShapeDtypeStruct(shape, LOW)] * 2,
        input_output_aliases=aliases,
        compiler_params=pltpu.CompilerParams(vmem_limit_bytes=SMALL_LIMIT),
        cost_estimate=cost(rank),
    )(scalars, *arrays)


def line_shape(seq_count):
    minor = 1
    while (2 * minor) ** 2 <= seq_count and seq_count % (2 * minor) == 0:
        minor *= 2
    return seq_count // minor, minor


def route(states, state_doc, state_pos, pieces, table):
    seq_count = lax.axis_size("seq")
    device = lax.axis_index("seq")
    row_count = states.shape[0]
    capacity = 3 * row_count // (4 * seq_count) + row_count // 16
    docs_all = state_doc.reshape(seq_count, row_count)
    positions_all = state_pos.reshape(seq_count, row_count)
    before = (
        lax.broadcasted_iota(jnp.int32, (row_count, row_count), 0)
        < lax.broadcasted_iota(jnp.int32, (row_count, row_count), 1)
    ).astype(LOW)
    own_docs = lax.dynamic_index_in_dim(docs_all, device, 0, keepdims=False)
    doc_ids = jnp.arange(seq_count, dtype=jnp.int32)
    own_hot = own_docs[None, :] == doc_ids[:, None]
    mine = docs_all == device
    ranks = jnp.dot(
        jnp.concatenate([own_hot, mine], axis=0).astype(LOW), before, preferred_element_type=WIDE
    ).astype(jnp.int32)
    own_ranks = jnp.sum(jnp.where(own_hot, ranks[:seq_count], 0), axis=0)
    targets = own_docs * capacity + own_ranks
    slots = jnp.arange(seq_count * capacity, dtype=jnp.int32)
    send_hot = (targets[None, :] == slots[:, None]).astype(LOW)
    piece_width = states.shape[1] // pieces
    arrived = []
    for piece in range(pieces):
        columns = states[:, piece * piece_width : (piece + 1) * piece_width]
        sent = jnp.dot(send_hot, columns, preferred_element_type=WIDE).astype(LOW)
        arrived.append(lax.all_to_all(sent, "seq", split_axis=0, concat_axis=0, tiled=True))
    arrival = jnp.where(mine, ranks[seq_count:], capacity)
    hit = arrival[:, None, :] == jnp.arange(capacity, dtype=jnp.int32)[None, :, None]
    slot_position = jnp.max(jnp.where(hit, positions_all[:, None, :], -1), axis=2).reshape(-1)
    place_hot = (
        slot_position[None, :] == jnp.arange(row_count, dtype=jnp.int32)[:, None]
    ).astype(LOW)
    arrived[0], table = lax.optimization_barrier((arrived[0], table))
    return [jnp.dot(place_hot, piece, preferred_element_type=WIDE).astype(LOW) for piece in arrived], table


def shards(
    queries, states, state_doc, state_pos, lengths, offsets, key_weight, value_weight, context_grad
):
    seq_count = lax.axis_size("seq")
    tp_count = lax.axis_size("tp")
    device = lax.axis_index("seq")
    part = lax.axis_index("tp")
    major, minor = line_shape(seq_count)
    z, x = device // minor, device % minor
    row_count = states.shape[0]
    feature_count = key_weight.shape[0]
    slice_width = feature_count // seq_count
    quarter = row_count // tp_count
    head_count = key_weight.shape[1] // HEAD_DIM
    group_count = 4
    heads = head_count // group_count
    width = heads * HEAD_DIM

    def at(major_index, minor_index):
        return major_index * minor + minor_index

    def step_up(value, first, last):
        pairs = [(at(i, j), at(i + 1, j)) for i in range(first, last) for j in range(minor)]
        return lax.ppermute(value, "seq", pairs)

    def step_down(value, first, last):
        pairs = [(at(i, j), at(i - 1, j)) for i in range(first, last) for j in range(minor)]
        return lax.ppermute(value, "seq", pairs)

    def turn(value, shift):
        pairs = [(at(i, j), at(i, (j + shift) % minor)) for i in range(major) for j in range(minor)]
        return lax.ppermute(value, "seq", pairs)

    pieces = seq_count // tp_count
    if minor % pieces or pieces > 2:
        pieces = 1
    def nearest(distance):
        return jnp.where(z + distance < major, z + distance, jnp.maximum(z - distance, 0))

    def dests_from(step):
        found = []
        for distance in range(major - step, 0, -1):
            if 2 * distance >= major:
                found.append(nearest(distance))
            else:
                found += [jnp.minimum(z + distance, major - 1), jnp.maximum(z - distance, 0)]
        return found + [z]

    first_dests, later_dests = [nearest(major - 1)], dests_from(2)
    side_dests = [(x + shift) % minor for shift in range(1, minor)] + [x]
    table = [
        lax.dynamic_index_in_dim(lengths, device, 0, keepdims=False),
        lax.dynamic_index_in_dim(offsets, device, 0, keepdims=False),
        z,
    ]
    z_slot = 2
    first_slot = len(table)
    table += [at(dest, x) // pieces for dest in first_dests] + first_dests
    later_slot = len(table)
    table += [at(dest, x) // pieces for dest in later_dests] + later_dests
    side_slot = len(table)
    table += side_dests
    table = jnp.stack([jnp.asarray(value, jnp.int32) for value in table])

    with jax.named_scope("route"):
        doc_pieces, table = route(states, state_doc, state_pos, pieces, table)
        doc_part = jnp.concatenate(doc_pieces, axis=1) if pieces > 1 else doc_pieces[0]

    ratio = tp_count // major
    slots = list(range(1, major, 2)) + list(range(2, major, 2)) + [0]
    piece_rows = row_count // ratio
    distance = jnp.asarray(slots, jnp.int32)[part // ratio]

    def send_line(states_of, piece):
        with jax.named_scope(f"line_states_{piece}"):
            rows = lax.dynamic_slice_in_dim(states_of, part % ratio * piece_rows, piece_rows, 0)
            found = [
                lax.dynamic_slice_in_dim(
                    rows, at((z + distance) % major, j) // pieces * slice_width, slice_width, 1
                )
                for j in range(piece, minor, pieces)
            ]
            rows = jnp.concatenate(found, axis=1) if len(found) > 1 else found[0]
            pairs = []
            for i in range(major):
                for j in range(minor):
                    for t in range(tp_count):
                        to = at((i + slots[t // ratio]) % major, j)
                        pairs.append((at(i, j) * tp_count + t, to * tp_count + t))
            return lax.ppermute(rows, ("seq", "tp"), pairs)

    side_parts = []
    if ratio == 1:
        with jax.named_scope("side_states"):
            for shift in range(1, minor):
                wanted = lax.dynamic_slice_in_dim(
                    doc_part, ((x + shift) % minor) * slice_width, slice_width, 1
                )
                side_parts.append(turn(wanted, shift))
    with jax.named_scope("gather_states"):
        doc_states = [lax.all_gather(piece, "tp", axis=1, tiled=True) for piece in doc_pieces]
    weight_shape = (tp_count, pieces, feature_count // (tp_count * pieces), key_weight.shape[1])
    key_parts, value_parts = key_weight.reshape(weight_shape), value_weight.reshape(weight_shape)
    found = [send_line(doc_states[piece], piece) for piece in range(pieces - 1)]
    partials = [None] * group_count
    if pieces == 2:
        with jax.named_scope("project_first_piece"):
            for group in range(group_count - 1):
                partials[group] = project_piece(
                    doc_states[0], 0, key_parts, value_parts, group * heads, heads
                )
    early = [value for value in partials if value is not None]
    joined = list(lax.optimization_barrier((*doc_states, *found, *side_parts, *early)))
    doc_states = [joined.pop(0) for _ in doc_states]
    found = [joined.pop(0) for _ in found]
    side_parts = [joined.pop(0) for _ in side_parts]
    if early:
        partials = [*joined, None]
    all_states = dict(enumerate(doc_states))
    late_states = {pieces - 1: doc_states[-1]}
    found.append(send_line(doc_states[-1], pieces - 1))

    def gather_line(after):
        with jax.named_scope("line_states"):
            pieces_found = lax.optimization_barrier((*found, after))[:-1]
            if 1 < pieces < minor:
                rows = [rows.reshape(piece_rows, minor // pieces, 1, slice_width) for rows in pieces_found]
                rows = jnp.concatenate(rows, axis=2).reshape(piece_rows, minor * slice_width)
            else:
                rows = jnp.concatenate(pieces_found, axis=1)
            return lax.all_gather(rows, "tp", axis=0, tiled=True)

    def piece_of(minor_index):
        if pieces == 1:
            return doc_states[0]
        return jnp.where(minor_index % 2 == 1, doc_states[1], doc_states[0])

    with jax.named_scope("side_states"):
        if ratio == 1:
            side_states = [
                lax.all_gather(piece, "tp", axis=0, tiled=True) for piece in side_parts
            ]
        else:
            side_states = []
            for shift in range(1, minor):
                own_rows = lax.dynamic_slice_in_dim(piece_of(x + shift), part * quarter, quarter, 0)
                wanted = jnp.concatenate(
                    [
                        lax.dynamic_slice_in_dim(
                            own_rows, at(i, (x + shift) % minor) // pieces * slice_width, slice_width, 1
                        )
                        for i in range(major)
                    ],
                    axis=1,
                )
                side_states.append(lax.all_gather(turn(wanted, shift), "tp", axis=0, tiled=True))
        own_states = piece_of(x)
    latest, pending, rank = None, [], 0

    def scalars():
        nonlocal rank
        rank += 1
        others = [] if latest is None else [latest]
        others += pending
        pending.clear()
        return lax.optimization_barrier((table, *others))[0]

    query_grads = [None] * group_count

    def attend_group(group):
        nonlocal latest
        with jax.named_scope(f"attend_{group}"):
            info = scalars()
            query_grads[group], latest = attend(
                rank, info, all_states if partials[group] is None else late_states, partials[group],
                key_parts, value_parts, queries, context_grad,
                group * heads, heads,
            )
            return latest

    even, odd = [None, None], [None, None]
    rows_up, rows_down = [[], []], [[], []]
    odd_rows = [None, None]
    sums_up, sums_down = [None, None], [None, None]
    side_own = [None, None]
    side_ahead, line_ahead, even_sums = [None, None], [None, None], [None, None]
    block = 4 * HEAD_DIM if heads % 2 == 0 else 2 * HEAD_DIM

    def send_first(index):
        with jax.named_scope(f"rows_0_{index}"):
            rows_up[index] = [(even[index], 0), (step_up(even[index], 0, major - 1), 0)]
            rows_down[index] = [(even[index], 0), (step_down(even[index], 1, major), 0)]

    def first_arrives(index):
        pending.extend([rows_up[index][1][0], rows_down[index][1][0]])

    def send_rows(step, index, before):
        nonlocal latest
        with jax.named_scope(f"rows_{step}_{index}"):
            up, down = rows_up[index][step][0], rows_down[index][step][0]
            others = [rows_up[before[1]][before[0] + 1][0], rows_down[before[1]][before[0] + 1][0]]
            if 2 * step < major:
                up, down = lax.optimization_barrier((up, down, latest, *others))[:2]
                up, down = step_up(up, step, major - 1), step_down(down, 1, major - step)
            else:
                pending.extend(others)
                info = scalars()
                latest = both = choose(rank, info, z_slot, step, up, down, block)
                pairs = [(at(i, j), at(i + 1, j)) for i in range(step, major - 1) for j in range(minor)]
                pairs += [(at(i, j), at(i - 1, j)) for i in range(1, major - step) for j in range(minor)]
                up = down = lax.ppermute(both, "seq", pairs)
            rows_up[index].append((up, 0))
            rows_down[index].append((down, 0))

    def send_odd(index):
        with jax.named_scope(f"side_rows_{index}"):
            odd_rows[index] = [odd[index]] + [turn(odd[index], shift) for shift in range(1, minor)]

    def side_products(index, slot, total, skip, count, free=False):
        nonlocal latest
        terms = [(own_states, lambda k, s: (0, s[slot + skip + k]), [(odd_rows[index][0], 0)], None)]
        for states_of, rows_of in zip(side_states, odd_rows[index][1:]):
            if ratio == 1:
                place = lambda k, s: (s[slot + total + skip + k], 0)
            else:
                place = lambda k, s: (0, s[slot + total + skip + k])
            terms.append((states_of, place, [(rows_of, 0)], None))
        info = scalars()
        found = products(0 if free else rank, info, z_slot, count, terms, row_count, slice_width, block)
        latest = found[-1]
        return found

    def send_sums(step, index):
        nonlocal latest
        distance = major - step
        up_pairs = [(at(i, j), at(i + 1, j)) for i in range(major - distance) for j in range(minor)]
        down_pairs = [(at(i, j), at(i - 1, j)) for i in range(distance, major) for j in range(minor)]
        with jax.named_scope(f"sums_{step}_{index}"):
            if step == 1:
                up = down = side_products(index, first_slot, 1, 0, 1)[0]
            else:
                place = len(later_dests) - len(dests_from(step))
                info = scalars()
                up, down = sums_up[index], sums_down[index]
                if up is down and 2 * distance >= major:
                    (up,) = add_arrivals(rank, info, [side_ahead[index][place]], [up], block)
                    down = up
                else:
                    bases = [side_ahead[index][place], side_ahead[index][place + (2 * distance < major)]]
                    up, down = add_arrivals(rank, info, bases, [up, down], block)
                latest = down
            if 2 * distance > major + 1 and up is down:
                sums_up[index] = sums_down[index] = lax.ppermute(up, "seq", up_pairs + down_pairs)
            else:
                sums_up[index] = lax.ppermute(up, "seq", up_pairs)
                sums_down[index] = lax.ppermute(down, "seq", down_pairs)

    def products_ahead(index):
        with jax.named_scope(f"side_ahead_{index}"):
            count = len(later_dests)
            if count > 1:
                side_ahead[index] = side_products(index, later_slot, count, 0, count - 1, True)

    def own_product(index, *awaited):
        with jax.named_scope(f"side_own_{index}"):
            pending.extend(awaited)
            count = len(later_dests)
            side_own[index] = side_products(index, later_slot, count, count - 1, 1)[0]

    def send_even(index):
        nonlocal latest
        with jax.named_scope(f"even_{index}"):
            terms = []
            for j in range(major):
                rights = [(even[index], 0)] if j == 0 else [rows_up[index][j], rows_down[index][major - j]]
                place = lambda k, s, slot=slots.index(j): (slot, s[side_slot + k])
                terms.append((line_states, place, rights, j if j else None))
            info = scalars()
            *sent, line_ahead[index] = products(
                rank, info, z_slot, minor, terms, row_count, slice_width, block
            )
            latest = line_ahead[index]
            even_sums[index] = [turn(value, shift) for shift, value in enumerate(sent, 1)]

    results = None
    steps = 2 * width // block

    def finish_group(addends, group):
        nonlocal latest, results
        with jax.named_scope(f"finish_{group}"):
            info = scalars()
            results = finish(
                rank, info, addends, results, (slice_width, key_weight.shape[1]), group * steps, block
            )
            latest = results[0]

    even[0] = attend_group(0)
    send_first(0)
    line_states = gather_line(latest)
    odd[0] = attend_group(2)
    send_odd(0)
    even[1] = attend_group(1)
    send_first(1)
    first_arrives(0)
    odd[1] = attend_group(3)
    send_odd(1)
    send_sums(1, 0)
    if major > 2:
        send_rows(1, 0, (0, 1))
    products_ahead(0)
    send_sums(1, 1)
    for step in range(2, major):
        if step > 2:
            send_rows(step - 1, 1, (step - 1, 0))
        send_sums(step, 0)
        if step == 2:
            send_rows(1, 1, (1, 0))
            products_ahead(1)
            own_product(1, sums_up[1], sums_down[1])
        if step < major - 1:
            send_rows(step, 0, (step - 1, 1))
        else:
            send_even(0)
        send_sums(step, 1)
        if step == 2:
            own_product(0, sums_up[0], sums_down[0])
    if major == 2:
        own_product(1)
        own_product(0)
        send_even(0)
    send_even(1)
    finish_group([side_own[0], sums_up[0], sums_down[0]], 2)
    finish_group([line_ahead[0], *even_sums[0]], 0)
    finish_group([side_own[1], sums_up[1], sums_down[1]], 3)
    finish_group([line_ahead[1], *even_sums[1]], 1)

    return (jnp.concatenate(query_grads, axis=1), *results)


def solution(mesh):
    in_specs = (
        P("seq", "tp"),
        P("seq", "tp"),
        P(),
        P(),
        P(),
        P(),
        P(None, "tp"),
        P(None, "tp"),
        P("seq", "tp"),
    )
    out_specs = (P("seq", "tp"), P("seq", "tp"), P("seq", "tp"))
    return jax.shard_map(shards, mesh=mesh, in_specs=in_specs, out_specs=out_specs, check_vma=False)
```

```python
import jax
import jax.numpy as jnp
from jax import lax
from jax.experimental import pallas as pl
from jax.experimental.pallas import tpu as pltpu
from jax.sharding import PartitionSpec as P

HEAD_DIM = 128
VMEM_LIMIT = 40 * 1024 * 1024
SMALL_LIMIT = 16 * 1024 * 1024


def cost(rank):
    return pl.CostEstimate(flops=0, bytes_accessed=rank * 2**19, transcendentals=0)
LOG2_E = 1.4426950408889634
LOW = jnp.bfloat16
WIDE = jnp.float32


def attend_kernel(pieces, info_ref, *refs):
    states_refs, key_refs, value_refs = refs[:pieces], refs[pieces : 2 * pieces], refs[2 * pieces : 3 * pieces]
    *partial_refs, query_ref, grad_ref, query_grad_ref, rows_grad_ref = refs[3 * pieces :]
    length = info_ref[0]
    offset = info_ref[1]
    scale = HEAD_DIM ** (-0.5)
    across = (((1,), (1,)), ((), ()))
    down = (((0,), (0,)), ((), ()))
    query_count, block = query_ref.shape
    state_count = states_refs[0].shape[0]

    def project(weight_refs, place):
        total = None
        for ref in partial_refs:
            total = ref[:, place * block : (place + 1) * block]
        for states_ref, weight_ref in zip(states_refs, weight_refs):
            weight = weight_ref[...].reshape(-1, block)
            product = jnp.dot(states_ref[...], weight, preferred_element_type=WIDE)
            total = product if total is None else total + product
        return total.astype(LOW)

    key_rows, value_rows = project(key_refs, 0), project(value_refs, 1)
    position = lax.broadcasted_iota(jnp.int32, (query_count, state_count), 1)
    limit = jnp.minimum(
        lax.broadcasted_iota(jnp.int32, (query_count, 1), 0) + (offset + 1), length
    )
    visible = position < limit
    heads = range(block // HEAD_DIM)
    columns = [slice(head * HEAD_DIM, (head + 1) * HEAD_DIM) for head in heads]
    query = [query_ref[:, part] for part in columns]
    grad = [grad_ref[:, part] for part in columns]
    key = [key_rows[:, part] for part in columns]
    value = [value_rows[:, part] for part in columns]

    def dots(left, right, dims):
        return [
            lax.dot_general(left[head], right[head], dims, preferred_element_type=WIDE) for head in heads
        ]

    scores = [jnp.where(visible, one, -1e30) for one in dots(query, key, across)]
    prob_grad = dots(grad, value, across)
    weights = [
        jnp.exp2((one - jnp.max(one, axis=-1, keepdims=True)) * (scale * LOG2_E)) for one in scores
    ]
    probs = [one * (1.0 / jnp.sum(one, axis=-1, keepdims=True)) for one in weights]
    probs_low = [one.astype(LOW) for one in probs]
    delta = [
        jnp.sum(probs_low[head].astype(WIDE) * prob_grad[head], axis=-1, keepdims=True) for head in heads
    ]
    score_grad = [
        (probs[head] * (prob_grad[head] - delta[head]) * scale).astype(LOW) for head in heads
    ]
    query_grads = dots(score_grad, key, (((1,), (0,)), ((), ())))
    key_grads = dots(query, score_grad, down)
    value_grads = dots(grad, probs_low, down)
    for head in heads:
        query_grad_ref[:, columns[head]] = query_grads[head].astype(LOW)
        rows_grad_ref[:, columns[head]] = key_grads[head].T.astype(LOW)
        value_columns = slice(block + head * HEAD_DIM, block + (head + 1) * HEAD_DIM)
        rows_grad_ref[:, value_columns] = value_grads[head].T.astype(LOW)


def attend(rank, info, states, partial, key_weight, value_weight, queries, grads, first, heads):
    query_count = queries.shape[0]
    numbers = sorted(states)
    state_count, feature_count = states[numbers[0]].shape
    part_count, _, part_features, _ = key_weight.shape
    pair = 2 if heads % 2 == 0 and first % 2 == 0 else 1
    block = pair * HEAD_DIM
    width = heads * HEAD_DIM
    weight_specs = [
        pl.BlockSpec(
            (part_count, 1, part_features, block), lambda h, piece=piece: (0, piece, 0, first // pair + h)
        )
        for piece in numbers
    ]
    states_spec = pl.BlockSpec(
        (state_count, feature_count), lambda h: (0, 0), pipeline_mode=pl.Buffered(1)
    )
    pieces = len(numbers)
    weights = [key_weight] * pieces + [value_weight] * pieces
    pair_spec = pl.BlockSpec((state_count, 2 * block), lambda h: (0, h))
    partials = [] if partial is None else [partial]
    return pl.pallas_call(
        lambda *refs: attend_kernel(pieces, *refs),
        grid=(heads // pair,),
        in_specs=[
            pl.BlockSpec(memory_space=pltpu.SMEM),
            *[states_spec] * pieces,
            *weight_specs,
            *weight_specs,
            *[pair_spec] * len(partials),
            pl.BlockSpec((query_count, block), lambda h: (0, first // pair + h)),
            pl.BlockSpec((query_count, block), lambda h: (0, first // pair + h)),
        ],
        out_specs=[pl.BlockSpec((query_count, block), lambda h: (0, h)), pair_spec],
        out_shape=[
            jax.ShapeDtypeStruct((query_count, width), LOW),
            jax.ShapeDtypeStruct((state_count, 2 * width), LOW),
        ],
        compiler_params=pltpu.CompilerParams(vmem_limit_bytes=40 * 1024 * 1024),
        cost_estimate=cost(rank),
    )(info, *[states[number] for number in numbers], *weights, *partials, queries, grads)


def project_piece(states, piece, key_weight, value_weight, first, heads):
    state_count, feature_count = states.shape
    part_count, _, part_features, _ = key_weight.shape
    pair = 2 if heads % 2 == 0 and first % 2 == 0 else 1
    block = pair * HEAD_DIM
    weight_spec = pl.BlockSpec(
        (part_count, 1, part_features, block), lambda h: (0, piece, 0, first // pair + h)
    )

    def body(states_ref, key_ref, value_ref, out_ref):
        for place, ref in enumerate((key_ref, value_ref)):
            weight = ref[...].reshape(-1, block)
            out_ref[:, place * block : (place + 1) * block] = jnp.dot(
                states_ref[...], weight, preferred_element_type=WIDE
            )

    return pl.pallas_call(
        body,
        grid=(heads // pair,),
        in_specs=[
            pl.BlockSpec((state_count, feature_count), lambda h: (0, 0), pipeline_mode=pl.Buffered(1)),
            weight_spec,
            weight_spec,
        ],
        out_specs=pl.BlockSpec((state_count, 2 * block), lambda h: (0, h)),
        out_shape=jax.ShapeDtypeStruct((state_count, 2 * heads * HEAD_DIM), WIDE),
        compiler_params=pltpu.CompilerParams(vmem_limit_bytes=40 * 1024 * 1024),
        cost_estimate=pl.CostEstimate(
            flops=4 * state_count * feature_count * heads * HEAD_DIM,
            bytes_accessed=4 * feature_count * heads * HEAD_DIM,
            transcendentals=0,
        ),
    )(states, key_weight, value_weight)


def products(rank, scalars, z_slot, count, terms, rows, slice_width, block):
    columns = terms[0][2][0][0].shape[1]
    arrays, specs = [], []
    for left, place, rights, _ in terms:
        for k in range(count):
            arrays.append(left)
            specs.append(pl.BlockSpec((rows, slice_width), lambda c, s, k=k, place=place: place(k, s)))
        for right, row in rights:
            arrays.append(right)
            specs.append(pl.BlockSpec((rows, block), lambda c, s, row=row: (row, c)))

    def body(scalar_ref, *refs):
        refs = list(refs)
        totals = [None] * count
        for _, _, rights, limit in terms:
            lefts = [refs.pop(0) for _ in range(count)]
            right = refs.pop(0)[...]
            if len(rights) == 2:
                right = jnp.where(scalar_ref[z_slot] >= limit, right, refs.pop(0)[...])
            for k in range(count):
                product = lax.dot_general(
                    lefts[k][...], right, (((0,), (0,)), ((), ())), preferred_element_type=WIDE
                )
                totals[k] = product if totals[k] is None else totals[k] + product
        for k in range(count):
            refs[k][...] = totals[k].astype(LOW)

    return pl.pallas_call(
        body,
        grid_spec=pltpu.PrefetchScalarGridSpec(
            num_scalar_prefetch=1,
            grid=(columns // block,),
            in_specs=specs,
            out_specs=[pl.BlockSpec((slice_width, block), lambda c, s: (0, c))] * count,
        ),
        out_shape=[jax.ShapeDtypeStruct((slice_width, columns), LOW)] * count,
        compiler_params=pltpu.CompilerParams(vmem_limit_bytes=VMEM_LIMIT),
        cost_estimate=cost(rank),
    )(scalars, *arrays)


def add_arrivals(rank, scalars, bases, arrivals, block):
    slice_width, columns = bases[0].shape
    count = len(bases)

    def body(scalar_ref, *refs):
        for base_ref, ref, out_ref in zip(refs[:count], refs[count:], refs[2 * count :]):
            out_ref[...] = (base_ref[...].astype(WIDE) + ref[...].astype(WIDE)).astype(LOW)

    flat = pl.BlockSpec((slice_width, block), lambda c, s: (0, c))
    return pl.pallas_call(
        body,
        grid_spec=pltpu.PrefetchScalarGridSpec(
            num_scalar_prefetch=1,
            grid=(columns // block,),
            in_specs=[flat] * (2 * count),
            out_specs=[flat] * count,
        ),
        out_shape=[jax.ShapeDtypeStruct((slice_width, columns), LOW)] * count,
        compiler_params=pltpu.CompilerParams(vmem_limit_bytes=SMALL_LIMIT),
        cost_estimate=cost(rank),
    )(scalars, *bases, *arrivals)


def choose(rank, scalars, z_slot, limit, up, down, block):
    rows, columns = up.shape

    def body(scalar_ref, up_ref, down_ref, out_ref):
        out_ref[...] = jnp.where(scalar_ref[z_slot] >= limit, up_ref[...], down_ref[...])

    spec = pl.BlockSpec((rows, block), lambda c, s: (0, c))
    return pl.pallas_call(
        body,
        grid_spec=pltpu.PrefetchScalarGridSpec(
            num_scalar_prefetch=1, grid=(columns // block,), in_specs=[spec] * 2, out_specs=spec
        ),
        out_shape=jax.ShapeDtypeStruct(up.shape, LOW),
        compiler_params=pltpu.CompilerParams(vmem_limit_bytes=SMALL_LIMIT),
        cost_estimate=cost(rank),
    )(scalars, up, down)


def finish(rank, scalars, addends, results, shape, first, block):
    slice_width, columns = addends[0].shape
    arrays = list(addends)
    specs = [pl.BlockSpec((slice_width, block), lambda c, s: (0, c))] * len(addends)
    aliases = {}
    if results is not None:
        aliases = {1 + len(arrays): 0, 2 + len(arrays): 1}
        arrays += list(results)
        specs += [pl.BlockSpec(memory_space=pl.ANY)] * 2

    def body(scalar_ref, *refs):
        total = refs[0][...].astype(WIDE)
        for ref in refs[1 : len(addends)]:
            total = total + ref[...].astype(WIDE)
        half = total.shape[1] // 2
        refs[-2][...] = total[:, :half].astype(LOW)
        refs[-1][...] = total[:, half:].astype(LOW)

    return pl.pallas_call(
        body,
        grid_spec=pltpu.PrefetchScalarGridSpec(
            num_scalar_prefetch=1,
            grid=(columns // block,),
            in_specs=specs,
            out_specs=[pl.BlockSpec((slice_width, block // 2), lambda c, s: (0, first + c))] * 2,
        ),
        out_shape=[jax.ShapeDtypeStruct(shape, LOW)] * 2,
        input_output_aliases=aliases,
        compiler_params=pltpu.CompilerParams(vmem_limit_bytes=SMALL_LIMIT),
        cost_estimate=cost(rank),
    )(scalars, *arrays)


def line_shape(seq_count):
    minor = 1
    while (2 * minor) ** 2 <= seq_count and seq_count % (2 * minor) == 0:
        minor *= 2
    return seq_count // minor, minor


def route(states, state_doc, state_pos, pieces, table):
    seq_count = lax.axis_size("seq")
    device = lax.axis_index("seq")
    row_count = states.shape[0]
    capacity = 3 * row_count // (4 * seq_count) + row_count // 16
    docs_all = state_doc.reshape(seq_count, row_count)
    positions_all = state_pos.reshape(seq_count, row_count)
    before = (
        lax.broadcasted_iota(jnp.int32, (row_count, row_count), 0)
        < lax.broadcasted_iota(jnp.int32, (row_count, row_count), 1)
    ).astype(LOW)
    own_docs = lax.dynamic_index_in_dim(docs_all, device, 0, keepdims=False)
    doc_ids = jnp.arange(seq_count, dtype=jnp.int32)
    own_hot = own_docs[None, :] == doc_ids[:, None]
    mine = docs_all == device
    ranks = jnp.dot(
        jnp.concatenate([own_hot, mine], axis=0).astype(LOW), before, preferred_element_type=WIDE
    ).astype(jnp.int32)
    own_ranks = jnp.sum(jnp.where(own_hot, ranks[:seq_count], 0), axis=0)
    targets = own_docs * capacity + own_ranks
    slots = jnp.arange(seq_count * capacity, dtype=jnp.int32)
    send_hot = (targets[None, :] == slots[:, None]).astype(LOW)
    piece_width = states.shape[1] // pieces
    arrived = []
    for piece in range(pieces):
        columns = states[:, piece * piece_width : (piece + 1) * piece_width]
        sent = jnp.dot(send_hot, columns, preferred_element_type=WIDE).astype(LOW)
        arrived.append(lax.all_to_all(sent, "seq", split_axis=0, concat_axis=0, tiled=True))
    arrival = jnp.where(mine, ranks[seq_count:], capacity)
    hit = arrival[:, None, :] == jnp.arange(capacity, dtype=jnp.int32)[None, :, None]
    slot_position = jnp.max(jnp.where(hit, positions_all[:, None, :], -1), axis=2).reshape(-1)
    place_hot = (
        slot_position[None, :] == jnp.arange(row_count, dtype=jnp.int32)[:, None]
    ).astype(LOW)
    arrived[0], table = lax.optimization_barrier((arrived[0], table))
    return [jnp.dot(place_hot, piece, preferred_element_type=WIDE).astype(LOW) for piece in arrived], table


def shards(
    queries, states, state_doc, state_pos, lengths, offsets, key_weight, value_weight, context_grad
):
    seq_count = lax.axis_size("seq")
    tp_count = lax.axis_size("tp")
    device = lax.axis_index("seq")
    part = lax.axis_index("tp")
    major, minor = line_shape(seq_count)
    z, x = device // minor, device % minor
    row_count = states.shape[0]
    feature_count = key_weight.shape[0]
    slice_width = feature_count // seq_count
    quarter = row_count // tp_count
    head_count = key_weight.shape[1] // HEAD_DIM
    group_count = 4
    heads = head_count // group_count
    width = heads * HEAD_DIM

    def at(major_index, minor_index):
        return major_index * minor + minor_index

    def step_up(value, first, last):
        pairs = [(at(i, j), at(i + 1, j)) for i in range(first, last) for j in range(minor)]
        return lax.ppermute(value, "seq", pairs)

    def step_down(value, first, last):
        pairs = [(at(i, j), at(i - 1, j)) for i in range(first, last) for j in range(minor)]
        return lax.ppermute(value, "seq", pairs)

    def turn(value, shift):
        pairs = [(at(i, j), at(i, (j + shift) % minor)) for i in range(major) for j in range(minor)]
        return lax.ppermute(value, "seq", pairs)

    pieces = seq_count // tp_count
    if minor % pieces or pieces > 2:
        pieces = 1
    def nearest(distance):
        return jnp.where(z + distance < major, z + distance, jnp.maximum(z - distance, 0))

    def dests_from(step):
        found = []
        for distance in range(major - step, 0, -1):
            if 2 * distance >= major:
                found.append(nearest(distance))
            else:
                found += [jnp.minimum(z + distance, major - 1), jnp.maximum(z - distance, 0)]
        return found + [z]

    first_dests, later_dests = [nearest(major - 1)], dests_from(2)
    side_dests = [(x + shift) % minor for shift in range(1, minor)] + [x]
    table = [
        lax.dynamic_index_in_dim(lengths, device, 0, keepdims=False),
        lax.dynamic_index_in_dim(offsets, device, 0, keepdims=False),
        z,
    ]
    z_slot = 2
    first_slot = len(table)
    table += [at(dest, x) // pieces for dest in first_dests] + first_dests
    later_slot = len(table)
    table += [at(dest, x) // pieces for dest in later_dests] + later_dests
    side_slot = len(table)
    table += side_dests
    table = jnp.stack([jnp.asarray(value, jnp.int32) for value in table])

    with jax.named_scope("route"):
        doc_pieces, table = route(states, state_doc, state_pos, pieces, table)
        doc_part = jnp.concatenate(doc_pieces, axis=1) if pieces > 1 else doc_pieces[0]

    ratio = tp_count // major
    slots = list(range(1, major, 2)) + list(range(2, major, 2)) + [0]
    piece_rows = row_count // ratio
    distance = jnp.asarray(slots, jnp.int32)[part // ratio]

    def send_line(states_of, piece):
        with jax.named_scope(f"line_states_{piece}"):
            rows = lax.dynamic_slice_in_dim(states_of, part % ratio * piece_rows, piece_rows, 0)
            found = [
                lax.dynamic_slice_in_dim(
                    rows, at((z + distance) % major, j) // pieces * slice_width, slice_width, 1
                )
                for j in range(piece, minor, pieces)
            ]
            rows = jnp.concatenate(found, axis=1) if len(found) > 1 else found[0]
            pairs = []
            for i in range(major):
                for j in range(minor):
                    for t in range(tp_count):
                        to = at((i + slots[t // ratio]) % major, j)
                        pairs.append((at(i, j) * tp_count + t, to * tp_count + t))
            return lax.ppermute(rows, ("seq", "tp"), pairs)

    side_parts = []
    if ratio == 1:
        with jax.named_scope("side_states"):
            for shift in range(1, minor):
                if pieces == minor == 2:
                    wanted = jnp.where((x + shift) % minor == 1, doc_pieces[1], doc_pieces[0])
                else:
                    wanted = lax.dynamic_slice_in_dim(
                        doc_part, ((x + shift) % minor) * slice_width, slice_width, 1
                    )
                side_parts.append(turn(wanted, shift))
    with jax.named_scope("gather_states"):
        doc_states = [lax.all_gather(piece, "tp", axis=1, tiled=True) for piece in doc_pieces]
    weight_shape = (tp_count, pieces, feature_count // (tp_count * pieces), key_weight.shape[1])
    key_parts, value_parts = key_weight.reshape(weight_shape), value_weight.reshape(weight_shape)
    found = [send_line(doc_states[piece], piece) for piece in range(pieces - 1)]
    partials = [None] * group_count
    if pieces == 2:
        with jax.named_scope("project_first_piece"):
            for group in range(group_count - 1):
                partials[group] = project_piece(
                    doc_states[0], 0, key_parts, value_parts, group * heads, heads
                )
    early = [value for value in partials if value is not None]
    joined = list(lax.optimization_barrier((*doc_states, *found, *side_parts, *early)))
    doc_states = [joined.pop(0) for _ in doc_states]
    found = [joined.pop(0) for _ in found]
    side_parts = [joined.pop(0) for _ in side_parts]
    if early:
        partials = [*joined, None]
    all_states = dict(enumerate(doc_states))
    late_states = {pieces - 1: doc_states[-1]}
    found.append(send_line(doc_states[-1], pieces - 1))

    def gather_line(after):
        with jax.named_scope("line_states"):
            pieces_found = lax.optimization_barrier((*found, after))[:-1]
            if 1 < pieces < minor:
                rows = [rows.reshape(piece_rows, minor // pieces, 1, slice_width) for rows in pieces_found]
                rows = jnp.concatenate(rows, axis=2).reshape(piece_rows, minor * slice_width)
            else:
                rows = jnp.concatenate(pieces_found, axis=1)
            return lax.all_gather(rows, "tp", axis=0, tiled=True)

    def piece_of(minor_index):
        if pieces == 1:
            return doc_states[0]
        return jnp.where(minor_index % 2 == 1, doc_states[1], doc_states[0])

    with jax.named_scope("side_states"):
        if ratio == 1:
            side_states = [
                lax.all_gather(piece, "tp", axis=0, tiled=True) for piece in side_parts
            ]
        else:
            side_states = []
            for shift in range(1, minor):
                own_rows = lax.dynamic_slice_in_dim(piece_of(x + shift), part * quarter, quarter, 0)
                wanted = jnp.concatenate(
                    [
                        lax.dynamic_slice_in_dim(
                            own_rows, at(i, (x + shift) % minor) // pieces * slice_width, slice_width, 1
                        )
                        for i in range(major)
                    ],
                    axis=1,
                )
                side_states.append(lax.all_gather(turn(wanted, shift), "tp", axis=0, tiled=True))
        own_states = piece_of(x)
    latest, pending, rank = None, [], 0

    def scalars():
        nonlocal rank
        rank += 1
        others = [] if latest is None else [latest]
        others += pending
        pending.clear()
        return lax.optimization_barrier((table, *others))[0]

    query_grads = [None] * group_count

    def attend_group(group):
        nonlocal latest
        with jax.named_scope(f"attend_{group}"):
            info = scalars()
            query_grads[group], latest = attend(
                rank, info, all_states if partials[group] is None else late_states, partials[group],
                key_parts, value_parts, queries, context_grad,
                group * heads, heads,
            )
            return latest

    even, odd = [None, None], [None, None]
    rows_up, rows_down = [[], []], [[], []]
    odd_rows = [None, None]
    sums_up, sums_down = [None, None], [None, None]
    side_own = [None, None]
    side_ahead, line_ahead, even_sums = [None, None], [None, None], [None, None]
    block = 4 * HEAD_DIM if heads % 2 == 0 else 2 * HEAD_DIM

    def send_first(index):
        with jax.named_scope(f"rows_0_{index}"):
            rows_up[index] = [(even[index], 0), (step_up(even[index], 0, major - 1), 0)]
            rows_down[index] = [(even[index], 0), (step_down(even[index], 1, major), 0)]

    def first_arrives(index):
        pending.extend([rows_up[index][1][0], rows_down[index][1][0]])

    def send_rows(step, index, before):
        nonlocal latest
        with jax.named_scope(f"rows_{step}_{index}"):
            up, down = rows_up[index][step][0], rows_down[index][step][0]
            others = [rows_up[before[1]][before[0] + 1][0], rows_down[before[1]][before[0] + 1][0]]
            if 2 * step < major:
                up, down = lax.optimization_barrier((up, down, latest, *others))[:2]
                up, down = step_up(up, step, major - 1), step_down(down, 1, major - step)
            else:
                pending.extend(others)
                info = scalars()
                latest = both = choose(rank, info, z_slot, step, up, down, block)
                pairs = [(at(i, j), at(i + 1, j)) for i in range(step, major - 1) for j in range(minor)]
                pairs += [(at(i, j), at(i - 1, j)) for i in range(1, major - step) for j in range(minor)]
                up = down = lax.ppermute(both, "seq", pairs)
            rows_up[index].append((up, 0))
            rows_down[index].append((down, 0))

    def send_odd(index):
        with jax.named_scope(f"side_rows_{index}"):
            odd_rows[index] = [odd[index]] + [turn(odd[index], shift) for shift in range(1, minor)]

    def side_products(index, slot, total, skip, count, free=False):
        nonlocal latest
        terms = [(own_states, lambda k, s: (0, s[slot + skip + k]), [(odd_rows[index][0], 0)], None)]
        for states_of, rows_of in zip(side_states, odd_rows[index][1:]):
            if ratio == 1:
                place = lambda k, s: (s[slot + total + skip + k], 0)
            else:
                place = lambda k, s: (0, s[slot + total + skip + k])
            terms.append((states_of, place, [(rows_of, 0)], None))
        info = scalars()
        found = products(0 if free else rank, info, z_slot, count, terms, row_count, slice_width, block)
        latest = found[-1]
        return found

    def send_sums(step, index):
        nonlocal latest
        distance = major - step
        up_pairs = [(at(i, j), at(i + 1, j)) for i in range(major - distance) for j in range(minor)]
        down_pairs = [(at(i, j), at(i - 1, j)) for i in range(distance, major) for j in range(minor)]
        with jax.named_scope(f"sums_{step}_{index}"):
            if step == 1:
                up = down = side_products(index, first_slot, 1, 0, 1)[0]
            else:
                place = len(later_dests) - len(dests_from(step))
                info = scalars()
                up, down = sums_up[index], sums_down[index]
                if up is down and 2 * distance >= major:
                    (up,) = add_arrivals(rank, info, [side_ahead[index][place]], [up], block)
                    down = up
                else:
                    bases = [side_ahead[index][place], side_ahead[index][place + (2 * distance < major)]]
                    up, down = add_arrivals(rank, info, bases, [up, down], block)
                latest = down
            if 2 * distance > major + 1 and up is down:
                sums_up[index] = sums_down[index] = lax.ppermute(up, "seq", up_pairs + down_pairs)
            else:
                sums_up[index] = lax.ppermute(up, "seq", up_pairs)
                sums_down[index] = lax.ppermute(down, "seq", down_pairs)

    def products_ahead(index):
        with jax.named_scope(f"side_ahead_{index}"):
            count = len(later_dests)
            if count > 1:
                side_ahead[index] = side_products(index, later_slot, count, 0, count - 1, True)

    def own_product(index, *awaited):
        with jax.named_scope(f"side_own_{index}"):
            pending.extend(awaited)
            count = len(later_dests)
            side_own[index] = side_products(index, later_slot, count, count - 1, 1)[0]

    def send_even(index):
        nonlocal latest
        with jax.named_scope(f"even_{index}"):
            terms = []
            for j in range(major):
                rights = [(even[index], 0)] if j == 0 else [rows_up[index][j], rows_down[index][major - j]]
                place = lambda k, s, slot=slots.index(j): (slot, s[side_slot + k])
                terms.append((line_states, place, rights, j if j else None))
            info = scalars()
            *sent, line_ahead[index] = products(
                rank, info, z_slot, minor, terms, row_count, slice_width, block
            )
            latest = line_ahead[index]
            even_sums[index] = [turn(value, shift) for shift, value in enumerate(sent, 1)]

    results = None
    steps = 2 * width // block

    def finish_group(addends, group):
        nonlocal latest, results
        with jax.named_scope(f"finish_{group}"):
            info = scalars()
            results = finish(
                rank, info, addends, results, (slice_width, key_weight.shape[1]), group * steps, block
            )
            latest = results[0]

    even[0] = attend_group(0)
    send_first(0)
    line_states = gather_line(latest)
    odd[0] = attend_group(2)
    send_odd(0)
    even[1] = attend_group(1)
    send_first(1)
    first_arrives(0)
    odd[1] = attend_group(3)
    send_odd(1)
    send_sums(1, 0)
    if major > 2:
        send_rows(1, 0, (0, 1))
    products_ahead(0)
    send_sums(1, 1)
    for step in range(2, major):
        if step > 2:
            send_rows(step - 1, 1, (step - 1, 0))
        send_sums(step, 0)
        if step == 2:
            send_rows(1, 1, (1, 0))
            products_ahead(1)
            own_product(1, sums_up[1], sums_down[1])
        if step < major - 1:
            send_rows(step, 0, (step - 1, 1))
        else:
            send_even(0)
        send_sums(step, 1)
        if step == 2:
            own_product(0, sums_up[0], sums_down[0])
    if major == 2:
        own_product(1)
        own_product(0)
        send_even(0)
    send_even(1)
    finish_group([side_own[0], sums_up[0], sums_down[0]], 2)
    finish_group([line_ahead[0], *even_sums[0]], 0)
    finish_group([side_own[1], sums_up[1], sums_down[1]], 3)
    finish_group([line_ahead[1], *even_sums[1]], 1)

    return (jnp.concatenate(query_grads, axis=1), *results)


def solution(mesh):
    in_specs = (
        P("seq", "tp"),
        P("seq", "tp"),
        P(),
        P(),
        P(),
        P(),
        P(None, "tp"),
        P(None, "tp"),
        P("seq", "tp"),
    )
    out_specs = (P("seq", "tp"), P("seq", "tp"), P("seq", "tp"))
    return jax.shard_map(shards, mesh=mesh, in_specs=in_specs, out_specs=out_specs, check_vma=False)
```
